32 devices in a mesh: gx: 8 (over z, x), gz: 4 (over y, core).
Axes of the slice: x: 2, y: 2, z: 4, core: 2. Of those that a mesh axis runs over, the one named last changes fastest.
Arguments:
- velocity: float32 [3, 256, 256, 128], P(None, 'gx', 'gz'), may hold values from -6 to 6
- rhs_old: float32 [3, 256, 256, 128], P(None, 'gx', 'gz'), may hold values from -6 to 6
Outputs:
- velocity_next: float32 [3, 256, 256, 128], P(None, 'gx', 'gz')
- convective: float32 [3, 256, 256, 128], P(None, 'gx', 'gz')
The draws below stay inside these ranges and needn't reach their ends.
All inputs are finite; a program needn't handle non-finite values.
Results may differ from the reference program's by a relative error of at most 0.00018.
Values sent between devices are 32-bit elements; how exact they have to be, the bound alone decides.
No kernel may reach another device: no remote copies, remote signals or barrier semaphores. Data moves between devices by JAX's collectives and lax.ppermute only.
A program may use at most 128 MiB of HBM per device.

```python
import jax
import jax.numpy as jnp
from jax import lax

CY = 128
NX = 256
NZ = 256
FILT = 64


def draw_velocity(key, part):
    subkeys = jax.random.split(jax.random.fold_in(key, 7), 3)
    extent = (3, NX, NZ, CY)
    position = jnp.arange(NX, dtype=jnp.float32) / NX
    amplitude = jax.random.uniform(subkeys[1], (3, 3, 1, NZ, CY), jnp.float32, 0.5, 1.5)
    phase_shift = jax.random.uniform(subkeys[2], (3, 3, 1, NZ, CY), jnp.float32, -jnp.pi, jnp.pi)
    wave_sum = jnp.zeros(extent, jnp.float32)
    for harmonic in range(3):
        phase_arg = 2.0 * jnp.pi * (harmonic + 1) * position[None, :, None, None] + phase_shift[harmonic]
        wave_sum = wave_sum + amplitude[harmonic] * jnp.sin(phase_arg) / (harmonic + 1)
    irregular = 0.7 * jax.random.truncated_normal(subkeys[0], -4.0, 4.0, extent, jnp.float32)
    mean_flow = jnp.array([1.0, 0.0, 0.4], jnp.float32).reshape(3, 1, 1, 1)
    return irregular + mean_flow + 0.5 * wave_sum


def shard_levels(rng, dims, cuts, low, top_value):
    def one(dim, shards_of):
        draws = jax.random.uniform(jax.random.fold_in(jax.random.fold_in(rng, 6), dim), (shards_of,), jnp.float32, low / len(cuts), top_value / len(cuts))
        return jnp.repeat(jnp.exp(draws), dims[dim] // shards_of).reshape((-1,) + (1,) * (len(dims) - dim - 1))

    factor_of = one(*cuts[0])
    for cut in cuts[1:]:
        factor_of = factor_of * one(*cut)
    return factor_of


def normal_values(stream_key, shape, scale, bound, cuts=(), held_as=jnp.bfloat16):
    level = shard_levels(stream_key, shape, cuts, -0.22, 0.18) if cuts else 1.0
    values = jax.random.normal(stream_key, shape, jnp.float32) * scale * level
    return jnp.minimum(jnp.maximum(values, -bound), bound).astype(held_as)


def setup_inputs(seed: int = 0) -> dict:
    key_list = jax.random.split(jax.random.key(seed), 3)
    velocity = draw_velocity(jax.random.fold_in(key_list[2], 71), 0)
    rhs_old = normal_values(key_list[1], (3, NX, NZ, CY), 1.0, 6.0, ((1, 8), (2, 4)), jnp.float32)
    return dict(velocity=velocity, rhs_old=rhs_old)


def gradients(field):
    along = 45.0 * (jnp.roll(field, -1, 0) - jnp.roll(field, 1, 0))
    along = along - 9.0 * (jnp.roll(field, -2, 0) - jnp.roll(field, 2, 0))
    along = (along + (jnp.roll(field, -3, 0) - jnp.roll(field, 3, 0))) / 60.0
    span = 45.0 * (jnp.roll(field, -1, 1) - jnp.roll(field, 1, 1))
    span = span - 9.0 * (jnp.roll(field, -2, 1) - jnp.roll(field, 2, 1))
    span = (span + (jnp.roll(field, -3, 1) - jnp.roll(field, 3, 1))) / 60.0
    return along, span


def filtered(field):
    count = field.shape[0]
    wave = 2.0 * jnp.pi * jnp.arange(count, dtype=field.dtype) / count
    strength = 1.0 * FILT * FILT
    symbol = 1.0 + 4.0 * strength * jnp.sin(0.5 * wave) ** 2
    spectrum = jnp.fft.fft(field, axis=0) / symbol[:, None, None]
    return jnp.real(jnp.fft.ifft(spectrum, axis=0)).astype(field.dtype)


def reference(velocity, rhs_old):
    along, span = lax.map(gradients, velocity)
    smooth = lax.map(filtered, velocity[0::2])
    convective = -(smooth[0:1] * along + smooth[1:2] * span)
    velocity_next = velocity + 0.5 * ((5.0 / 12.0) * convective - (17.0 / 60.0) * rhs_old)
    return velocity_next, convective
```

```python
import functools
import math

import jax
import jax.numpy as jnp
import numpy as np
from jax import lax
from jax.experimental import pallas as pl
from jax.experimental.pallas import tpu as pltpu
from jax.sharding import PartitionSpec as P

TAPS = ((1, 45.0), (2, -9.0), (3, 1.0))
REACH = 3
PAD = 8
VMEM_LIMIT = 56 * 1024 * 1024


def decay_of(coupling):
    ratio = 0.5 / math.sqrt(coupling)
    theta = 2.0 * math.log(ratio + math.sqrt(ratio * ratio + 1.0))
    return theta, 1.0 / (coupling * (math.exp(theta) - math.exp(-theta)))


def round_tables(count, blocks, theta, gain):
    rounds = blocks.bit_length() - 1
    wrap = gain / (1.0 - math.exp(-theta * count * blocks))
    power = lambda steps: math.exp(-theta * count * steps)
    final = np.zeros((blocks, rounds + 1, 2))
    merge = np.zeros((blocks, rounds, 2, 2))
    for block in range(blocks):
        final[block, 0] = wrap * power(blocks - 1)
        for k in range(rounds):
            size = 1 << k
            start = ((block >> k) ^ 1) << k
            final[block, k + 1, 0] = wrap * power((block - start - size) % blocks)
            final[block, k + 1, 1] = wrap * power((start - 1 - block) % blocks)
            at_right = start > block
            merge[block, k, 0] = (power(size), 1.0) if at_right else (1.0, power(size))
            merge[block, k, 1] = (1.0, power(size)) if at_right else (power(size), 1.0)
    return final, merge


def pack_kernel(theta, v_hbm, fg, head, tail, zhead, ztail, v, sems):
    count, rows, lanes = v.shape[1:]
    chunk = 8
    copies = []
    for part in range(count // chunk):
        where = pl.ds(part * chunk, chunk)
        copy = pltpu.make_async_copy(v_hbm.at[:, where], v.at[:, where], sems.at[part])
        copy.start()
        copies.append(copy)
    for part, copy in enumerate(copies):
        copy.wait()
        for m in range(2):
            first = fg[m] if part else jnp.zeros((rows, lanes), jnp.float32)
            last = fg[2 + m] if part else jnp.zeros((rows, lanes), jnp.float32)
            for j in range(part * chunk, (part + 1) * chunk):
                cell = v[2 * m, j]
                first = first * math.exp(-theta) + cell
                last = last + cell * math.exp(-theta * j)
            fg[m] = first
            fg[2 + m] = last
        for c in range(3):
            if part == 0:
                head[c] = v[c, 0:REACH]
            if part == len(copies) - 1:
                tail[c] = v[c, count - REACH :]
    flat = v.reshape(3 * count * rows, lanes)
    for c in range(3):
        for k in range(REACH):
            zhead[k, c] = flat[pl.ds(c * count * rows + k, count, stride=rows), :]
            ztail[k, c] = flat[pl.ds(c * count * rows + rows - REACH + k, count, stride=rows), :]


def middle_kernel(theta, gain, v_hbm, rhs_hbm, zleft, zright, along, span, local, base, v, rhs, sems):
    count, rows, lanes = rhs.shape[1:]
    copies = []
    for c in range(3):
        copies.append(
            pltpu.make_async_copy(v_hbm.at[c], v.at[c, :, pl.ds(PAD, rows)], sems.at[c])
        )
        copies.append(pltpu.make_async_copy(rhs_hbm.at[c], rhs.at[c], sems.at[3 + c]))
    for copy in copies:
        copy.start()
    for copy in copies:
        copy.wait()
    deep = rows + 2 * PAD
    flat = v.reshape(3 * count * deep, lanes)
    for c in range(3):
        for k in range(REACH):
            flat[pl.ds(c * count * deep + PAD - REACH + k, count, stride=deep), :] = zleft[k, c]
            flat[pl.ds(c * count * deep + PAD + rows + k, count, stride=deep), :] = zright[k, c]
    here = pl.ds(PAD, rows)
    for c in range(3):

        def plane(x, carry, c=c):
            total = None
            for reach, tap in TAPS:
                diff = v[c, x, pl.ds(PAD + reach, rows)] - v[c, x, pl.ds(PAD - reach, rows)]
                total = diff * (-tap / 60.0) if total is None else total + diff * (-tap / 60.0)
            span[c, x] = total
            base[c, x] = v[c, x, here] - rhs[c, x] * (17.0 / 120.0)
            return carry

        lax.fori_loop(0, count, plane, 0)

        def inner(x, carry, c=c):
            total = None
            for reach, tap in TAPS:
                diff = v[c, x + reach, here] - v[c, x - reach, here]
                total = diff * (-tap / 60.0) if total is None else total + diff * (-tap / 60.0)
            along[c, x] = total
            return carry

        lax.fori_loop(REACH, count - REACH, inner, 0)
        for x in (*range(REACH), *range(count - REACH, count)):
            total = None
            for reach, tap in TAPS:
                for side in (-1, 1):
                    if 0 <= x + side * reach < count:
                        term = v[c, x + side * reach, here] * (-side * tap / 60.0)
                        total = term if total is None else total + term
            along[c, x] = total
    ratio = math.exp(-theta)
    for m in range(2):

        def forward(x, run, m=m):
            run = run * ratio + v[2 * m, x, here]
            local[m, x] = run * gain
            return run

        lax.fori_loop(0, count, forward, jnp.zeros((rows, lanes), jnp.float32))

        def backward(i, run, m=m):
            x = count - 1 - i
            local[m, x] = local[m, x] + run * gain
            return (run + v[2 * m, x, here]) * ratio

        lax.fori_loop(0, count, backward, jnp.zeros((rows, lanes), jnp.float32))


def final_kernel(rounds, weights, decay, *refs):
    received = refs[: rounds + 1]
    left, right, along, span, local, base, new, conv, inflow = refs[rounds + 1 :]
    step = pl.program_id(0)
    steps = pl.num_programs(0)
    planes = conv.shape[1]

    @pl.when(step == 0)
    def _():
        for side in range(2):
            for m in range(2):
                total = None
                for k in range(rounds + 1):
                    term = received[k][2 * side + m] * weights[k, side]
                    total = term if total is None else total + term
                inflow[2 * side + m] = total

    def planes_of(extra):
        for i in range(planes):
            x = step * planes + i
            rise, fall = decay[0, x], decay[1, x]
            smooth = [
                local[m, x] + inflow[m] * rise + inflow[2 + m] * fall for m in range(2)
            ]
            for c in range(3):
                gradient = along[c, x]
                for ref, index, factor in extra(i):
                    gradient = gradient + ref[c, index] * factor
                value = smooth[0] * gradient + smooth[1] * span[c, x]
                conv[c, i] = value
                new[c, i] = base[c, x] + value * (5.0 / 24.0)

    def at_left(i):
        return [(left, i - reach + REACH, tap / 60.0) for reach, tap in TAPS if i - reach < 0]

    def at_right(i):
        return [
            (right, i + reach - planes, -tap / 60.0) for reach, tap in TAPS if i + reach >= planes
        ]

    pl.when(step == 0)(lambda: planes_of(at_left))
    pl.when(step == steps - 1)(lambda: planes_of(at_right))
    pl.when((step > 0) & (step < steps - 1))(lambda: planes_of(lambda i: []))


def per_device(velocity, rhs_old):
    _, count, rows, lanes = velocity.shape
    blocks = lax.axis_size("gx")
    spans = lax.axis_size("gz")
    rounds = blocks.bit_length() - 1
    assert blocks == 1 << rounds
    filter_cells = count * blocks // 4
    theta, gain = decay_of(1.0 * filter_cells * filter_cells)
    f32 = jnp.float32
    shape = lambda *dims: jax.ShapeDtypeStruct(dims, f32)
    vmem = pl.BlockSpec(memory_space=pltpu.VMEM)
    smem = pl.BlockSpec(memory_space=pltpu.SMEM)
    anywhere = pl.BlockSpec(memory_space=pl.ANY)
    params = pltpu.CompilerParams(vmem_limit_bytes=VMEM_LIMIT)

    fg, head, tail, zhead, ztail = pl.pallas_call(
        functools.partial(pack_kernel, theta),
        out_shape=[
            shape(4, rows, lanes),
            shape(3, REACH, rows, lanes),
            shape(3, REACH, rows, lanes),
            shape(REACH, 3, count, lanes),
            shape(REACH, 3, count, lanes),
        ],
        in_specs=[anywhere],
        out_specs=[vmem] * 5,
        scratch_shapes=[pltpu.VMEM(velocity.shape, f32), pltpu.SemaphoreType.DMA((count // 8,))],
        compiler_params=params,
        name="pack",
    )(velocity)

    final, merge = round_tables(count, blocks, theta, gain)
    block = lax.axis_index("gx")
    weights = lax.dynamic_index_in_dim(jnp.asarray(final, f32), block, 0, keepdims=False)
    mixes = lax.dynamic_index_in_dim(jnp.asarray(merge, f32), block, 0, keepdims=False)
    ring = lambda axis, step: [(i, (i + step) % lax.axis_size(axis)) for i in range(lax.axis_size(axis))]

    received = [fg]
    held = fg
    for k in range(rounds):
        got = lax.ppermute(held, "gx", [(i, i ^ (1 << k)) for i in range(blocks)])
        received.append(got)
        if k < rounds - 1:
            own = jnp.repeat(mixes[k, :, 0], 2)[:, None, None]
            other = jnp.repeat(mixes[k, :, 1], 2)[:, None, None]
            held = held * own + got * other
    zleft = lax.ppermute(ztail, "gz", ring("gz", 1))
    zright = lax.ppermute(zhead, "gz", ring("gz", -1))
    left = lax.ppermute(tail, "gx", ring("gx", 1))
    right = lax.ppermute(head, "gx", ring("gx", -1))

    along, span, local, base = pl.pallas_call(
        functools.partial(middle_kernel, theta, gain),
        out_shape=[shape(*velocity.shape)] * 2 + [shape(2, count, rows, lanes), shape(*velocity.shape)],
        in_specs=[anywhere, anywhere, vmem, vmem],
        out_specs=[vmem] * 4,
        scratch_shapes=[
            pltpu.VMEM((3, count, rows + 2 * PAD, lanes), f32),
            pltpu.VMEM(velocity.shape, f32),
            pltpu.SemaphoreType.DMA((6,)),
        ],
        compiler_params=params,
        name="middle",
    )(velocity, rhs_old, zleft, zright)

    steps = theta * np.arange(1, count + 1)
    decay = jnp.asarray(np.stack([np.exp(-steps), np.exp(-steps[::-1])]), f32)
    planes = 4
    out = pl.BlockSpec((3, planes, rows, lanes), lambda i: (0, i, 0, 0))
    return pl.pallas_call(
        functools.partial(final_kernel, rounds),
        grid=(count // planes,),
        out_shape=[shape(*velocity.shape)] * 2,
        in_specs=[smem, smem] + [vmem] * (rounds + 1 + 6),
        out_specs=[out, out],
        scratch_shapes=[pltpu.VMEM((4, rows, lanes), f32)],
        compiler_params=params,
        name="final",
    )(weights, decay, *received, left, right, along, span, local, base)


def solution(mesh):
    placed = P(None, "gx", "gz", None)
    return jax.shard_map(
        lambda velocity, rhs_old: tuple(per_device(velocity, rhs_old)),
        mesh=mesh,
        in_specs=(placed, placed),
        out_specs=(placed, placed),
        check_vma=False,
    )
```

```python
import functools
import math

import jax
import jax.numpy as jnp
import numpy as np
from jax import lax
from jax.experimental import pallas as pl
from jax.experimental.pallas import tpu as pltpu
from jax.sharding import PartitionSpec as P

TAPS = ((1, 45.0), (2, -9.0), (3, 1.0))
REACH = 3
TILE = 8
MIB = 1024 * 1024
F32 = jnp.float32


def decay_of(coupling):
    ratio = 0.5 / math.sqrt(coupling)
    theta = 2.0 * math.log(ratio + math.sqrt(ratio * ratio + 1.0))
    return theta, 1.0 / (coupling * (math.exp(theta) - math.exp(-theta)))


def round_table(count, blocks, theta, gain):
    rounds = blocks.bit_length() - 1
    wrap = gain / (1.0 - math.exp(-theta * count * blocks))
    factor = lambda steps: math.exp(-theta * count * (steps % blocks))
    table = np.zeros((blocks, 2 + 4 * (rounds - 1), 4))
    for block in range(blocks):
        takers = (block, block ^ 1)
        for i, taker in enumerate(takers):
            table[block, i, :2] = wrap * factor(taker - 1 - block)
            table[block, i, 2:] = wrap * factor(block - taker - 1)
        for k in range(1, rounds):
            size = 1 << (k - 1)
            start = ((block >> k) ^ 1) << (k - 1)
            lowest = 2 * start + (block & 1)
            highest = lowest + 2 * (size - 1)
            slot = 4 * k - 2
            shrink = math.exp(-theta * count * 2 * size)
            at_right = lowest > block
            table[block, slot] = (shrink, shrink, 1.0, 1.0) if at_right else (1.0, 1.0, shrink, shrink)
            table[block, slot + 1] = (1.0, 1.0, shrink, shrink) if at_right else (shrink, shrink, 1.0, 1.0)
            for i, taker in enumerate(takers):
                table[block, slot + 2 + i, :2] = wrap * factor(taker - 1 - highest)
                table[block, slot + 2 + i, 2:] = wrap * factor(lowest - taker - 1)
    return table


def scaled(table, slot, part, value):
    return value * table[slot, pl.ds(part, 1)]


def sums_kernel(theta, v_hbm, odd, fg, near_x, far_x, v, ends, sems, strip_sems):
    count, rows, lanes = v.shape[1:]
    chunk = TILE
    parts = count // chunk
    copies = {}
    for part in range(parts):
        for m in range(2):
            where = pl.ds(part * chunk, chunk)
            copies[part, m] = pltpu.make_async_copy(
                v_hbm.at[2 * m, where], v.at[m, where], sems.at[m, part]
            )
            copies[part, m].start()
    strips = []
    for i, start in enumerate((0, count - REACH)):
        strips.append(
            pltpu.make_async_copy(v_hbm.at[:, pl.ds(start, REACH)], ends.at[i], strip_sems.at[i])
        )
        strips[-1].start()
    for part in range(parts):
        for m in range(2):
            copies[part, m].wait()
            first = fg[m] if part else jnp.zeros((rows, lanes), F32)
            last = fg[2 + m] if part else jnp.zeros((rows, lanes), F32)
            for j in range(part * chunk, (part + 1) * chunk):
                cell = v[m, j]
                first = first * math.exp(-theta) + cell
                last = last + cell * math.exp(-theta * j)
            fg[m] = first
            fg[2 + m] = last
    for copy in strips:
        copy.wait()
    at_odd = odd[0:1] > 0.0
    for c in range(3):
        for k in range(REACH):
            near_x[c, k] = jnp.where(at_odd, ends[0, c, k], ends[1, c, k])
            far_x[c, k] = jnp.where(at_odd, ends[1, c, k], ends[0, c, k])


def merge_kernel(k, table, held, got, after, out):
    del after
    for part in range(4):
        out[part] = scaled(table, 4 * k - 2, part, held[part]) + scaled(table, 4 * k - 1, part, got[part])


def flow(table, which, fg, received, part):
    total = scaled(table, which, part, fg[part])
    for k, got in enumerate(received, 1):
        total = total + scaled(table, 4 * k + which, part, got[part])
    return total


def outflow_kernel(rounds, table, fg, *refs):
    received, out = refs[: rounds - 1], refs[-1]
    for part in range(4):
        out[part] = flow(table, 1, fg, received, part)


def pack_kernel(v, zhead, ztail):
    count, rows, lanes = v.shape[1:]
    flat = v.reshape(3 * count * rows, lanes)
    for target, base in ((zhead, 0), (ztail, rows - REACH)):
        for c in range(3):
            for k in range(REACH):
                target[k, c] = flat[pl.ds(c * count * rows + base + k, count, stride=rows), :]


def local_kernel(theta, gain, v, local):
    count, rows, lanes = v.shape[1:]
    ratio = math.exp(-theta)
    for m in range(2):

        def forward(x, run, m=m):
            run = run * ratio + v[2 * m, x]
            local[m, x] = run * gain
            return run

        lax.fori_loop(0, count, forward, jnp.zeros((rows, lanes), F32), unroll=4)

        def backward(i, run, m=m):
            x = count - 1 - i
            local[m, x] = local[m, x] + run * gain
            return (run + v[2 * m, x]) * ratio

        lax.fori_loop(0, count, backward, jnp.zeros((rows, lanes), F32), unroll=4)


def along_kernel(v, rhs, near_got, odd, inner, rim, base):
    count = v.shape[1]
    at_odd = odd[0:1]
    for c in range(3):

        def plane(x, carry, c=c):
            total = None
            for reach, tap in TAPS:
                term = (v[c, x + REACH + reach] - v[c, x + REACH - reach]) * (-tap / 60.0)
                total = term if total is None else total + term
            inner[c, x] = total
            return carry

        lax.fori_loop(0, count - 2 * REACH, plane, 0, unroll=2)
        for i, x in enumerate((*range(REACH), *range(count - REACH, count))):
            total = None
            share = at_odd if i < REACH else 1.0 - at_odd
            for reach, tap in TAPS:
                for side in (-1, 1):
                    at = x + side * reach
                    if 0 <= at < count:
                        term = v[c, at] * (-side * tap / 60.0)
                    else:
                        term = near_got[c, at % count % (count - REACH)] * (share * (-side * tap / 60.0))
                    total = term if total is None else total + term
            rim[c, i] = total

        def rest(x, carry, c=c):
            base[c, x] = v[c, x] - rhs[c, x] * (17.0 / 120.0)
            return carry

        lax.fori_loop(0, count, rest, 0, unroll=4)


def span_kernel(v, zleft, zright, span, low, high):
    count, rows, lanes = v.shape[1:]
    deep = 3 * TILE

    def differences(ref, lead, start, size):
        total = None
        for reach, tap in TAPS:
            up = ref[(*lead, pl.ds(start + reach, size))]
            down = ref[(*lead, pl.ds(start - reach, size))]
            term = (up - down) * (-tap / 60.0)
            total = term if total is None else total + term
        return total

    for c in range(3):
        for k in range(REACH):
            low.reshape(3 * count * deep, lanes)[
                pl.ds(c * count * deep + TILE - REACH + k, count, stride=deep), :
            ] = zleft[k, c]
            high.reshape(3 * count * deep, lanes)[
                pl.ds(c * count * deep + 2 * TILE + k, count, stride=deep), :
            ] = zright[k, c]

        def plane(x, carry, c=c):
            low[c, x, pl.ds(TILE, 2 * TILE)] = v[c, x, pl.ds(0, 2 * TILE)]
            high[c, x, pl.ds(0, 2 * TILE)] = v[c, x, pl.ds(rows - 2 * TILE, 2 * TILE)]
            span[c, x, pl.ds(TILE, rows - 2 * TILE)] = differences(v, (c, x), TILE, rows - 2 * TILE)
            span[c, x, pl.ds(0, TILE)] = differences(low, (c, x), TILE, TILE)
            span[c, x, pl.ds(rows - TILE, TILE)] = differences(high, (c, x), TILE, TILE)
            return carry

        lax.fori_loop(0, count, plane, 0, unroll=2)


def final_kernel(theta, rounds, table, odd, fg, *refs):
    received, mate = refs[: rounds - 1], refs[rounds - 1]
    far_got, inner, rim, span, local, base, new, conv, inflow, new_out, conv_out, sems = refs[rounds:]
    count = span.shape[1]
    chunk = 2
    ratio = math.exp(-theta)
    for part in range(4):
        inflow[part] = flow(table, 0, fg, received, part) + mate[part]

    def plane(x, rise, fall, gradients):
        smooth = [local[m, x] + inflow[m] * rise + inflow[2 + m] * fall for m in range(2)]
        for c in range(3):
            value = smooth[0] * gradients(c) + smooth[1] * span[c, x]
            conv_out[c, x] = value
            new_out[c, x] = base[c, x] + value * (5.0 / 24.0)

    def copies(x, size, sem):
        where = pl.ds(x, size)
        return [
            pltpu.make_async_copy(staged.at[:, where], out.at[:, where], sems.at[i, sem])
            for i, (staged, out) in enumerate(((new_out, new), (conv_out, conv)))
        ]

    chunks = (count - 2 * REACH) // chunk

    def body(i, carry):
        rise, fall = carry
        for at in range(chunk):
            x = REACH + i * chunk + at
            plane(x, rise * ratio**at, fall * ratio**-at, lambda c: inner[c, x - REACH])
        for copy in copies(REACH + i * chunk, chunk, i):
            copy.start()
        return rise * ratio**chunk, fall * ratio**-chunk

    lax.fori_loop(
        0,
        chunks,
        body,
        (jnp.float32(ratio ** (REACH + 1)), jnp.float32(ratio ** (count - REACH))),
    )
    for side, start in enumerate((0, count - REACH)):
        for at in range(REACH):
            x = start + at

            def gradients(c):
                total = rim[c, side * REACH + at]
                share = odd[0:1] if side else 1.0 - odd[0:1]
                for reach, tap in TAPS:
                    if x - reach < 0:
                        total = total + far_got[c, x - reach + REACH] * (share * (tap / 60.0))
                    if x + reach >= count:
                        total = total + far_got[c, x + reach - count] * (share * (-tap / 60.0))
                return total

            plane(x, ratio ** (x + 1), ratio ** (count - x), gradients)
        for copy in copies(start, REACH, chunks + side):
            copy.start()
    for i in range(chunks):
        for copy in copies(REACH + i * chunk, chunk, i):
            copy.wait()
    for side, start in enumerate((0, count - REACH)):
        for copy in copies(start, REACH, chunks + side):
            copy.wait()


def per_device(velocity, rhs_old):
    _, count, rows, lanes = velocity.shape
    blocks = lax.axis_size("gx")
    rounds = blocks.bit_length() - 1
    assert blocks == 1 << rounds
    filter_cells = count * blocks // 4
    theta, gain = decay_of(1.0 * filter_cells * filter_cells)
    kept = lambda *dims: pltpu.VMEM(dims, F32)
    near = lambda *arrays: [pltpu.with_memory_space_constraint(a, pltpu.VMEM) for a in arrays]
    far = lambda *arrays: [pltpu.with_memory_space_constraint(a, pltpu.HBM) for a in arrays]
    vmem = pl.BlockSpec(memory_space=pltpu.VMEM)
    hbm = pl.BlockSpec(memory_space=pltpu.HBM)
    dma = pltpu.SemaphoreType.DMA

    def call(kernel, name, inputs, in_specs, outputs, out_spec, scratch, mib):
        return pl.pallas_call(
            kernel,
            out_shape=outputs,
            in_specs=in_specs,
            out_specs=[out_spec] * len(outputs),
            scratch_shapes=scratch,
            compiler_params=pltpu.CompilerParams(vmem_limit_bytes=mib * MIB),
            name=name,
        )(*inputs)

    full = velocity.shape
    block = lax.axis_index("gx")
    odd = jnp.broadcast_to((block & 1).astype(F32), (TILE, lanes))
    entries = round_table(count, blocks, theta, gain)
    slots = entries.shape[1]
    table = lax.dynamic_index_in_dim(jnp.asarray(entries, F32), block, 0, keepdims=False)
    table = jnp.broadcast_to(table[:, :, None], (slots, 4, lanes))
    flip = lambda bit: [(i, i ^ bit) for i in range(blocks)]
    beyond = [(i, (i - 1 + 2 * (i % 2)) % blocks) for i in range(blocks)]
    ring = lambda axis, step: [(i, (i + step) % lax.axis_size(axis)) for i in range(lax.axis_size(axis))]

    fg, near_x, far_x = call(
        functools.partial(sums_kernel, theta),
        "sums",
        far(velocity) + near(odd),
        [hbm, vmem],
        [kept(4, rows, lanes)] + [kept(3, REACH, rows, lanes)] * 2,
        vmem,
        [
            pltpu.VMEM((2, count, rows, lanes), F32),
            pltpu.VMEM((2, 3, REACH, rows, lanes), F32),
            dma((2, count // TILE)),
            dma((2,)),
        ],
        6,
    )
    velocity_near, fg = lax.optimization_barrier((velocity, fg))
    zhead, ztail = call(
        pack_kernel, "pack", near(velocity_near), [vmem], [kept(REACH, 3, count, lanes)] * 2, vmem, [], 2
    )
    (local,) = call(
        functools.partial(local_kernel, theta, gain),
        "local",
        near(velocity_near),
        [vmem],
        [kept(2, *full[1:])],
        vmem,
        [],
        2,
    )
    received = [lax.ppermute(fg, "gx", flip(2))]
    near_got = lax.ppermute(near_x, "gx", flip(1))
    zleft = lax.ppermute(ztail, "gz", ring("gz", 1))
    zright = lax.ppermute(zhead, "gz", ring("gz", -1))
    held, after = fg, local
    for k in range(1, rounds - 1):
        (held,) = call(
            functools.partial(merge_kernel, k),
            "merge",
            near(table, held, received[-1], after),
            [vmem] * 4,
            [kept(4, rows, lanes)],
            vmem,
            [],
            2,
        )
        if k == 1:
            held, far_x = lax.optimization_barrier((held, far_x))
        received.append(lax.ppermute(held, "gx", flip(2 << k)))
    far_got = lax.ppermute(far_x, "gx", beyond)
    (span,) = call(
        span_kernel,
        "span",
        near(velocity_near, zleft, zright),
        [vmem] * 3,
        [kept(*full)],
        vmem,
        [pltpu.VMEM((3, count, 3 * TILE, lanes), F32)] * 2,
        5,
    )
    inner, rim, base = call(
        along_kernel,
        "along",
        near(velocity_near, rhs_old, near_got, odd),
        [vmem] * 4,
        [kept(3, count - 2 * REACH, rows, lanes), kept(3, 2 * REACH, rows, lanes), kept(*full)],
        vmem,
        [],
        2,
    )
    (outflow,) = call(
        functools.partial(outflow_kernel, rounds),
        "outflow",
        near(table, fg, *received, span, rim),
        [vmem] * (rounds + 3),
        [kept(4, rows, lanes)],
        vmem,
        [],
        2,
    )
    mate = lax.ppermute(outflow, "gx", flip(1))
    inputs = near(table, odd, fg, *received, mate, far_got, inner, rim, span, local, base)
    return call(
        functools.partial(final_kernel, theta, rounds),
        "final",
        inputs,
        [vmem] * len(inputs),
        [jax.ShapeDtypeStruct(full, F32)] * 2,
        hbm,
        [pltpu.VMEM((4, rows, lanes), F32)]
        + [pltpu.VMEM(full, F32)] * 2
        + [dma((2, (count - 2 * REACH) // 2 + 2))],
        8,
    )


def solution(mesh):
    placed = P(None, "gx", "gz", None)
    return jax.shard_map(
        lambda velocity, rhs_old: tuple(per_device(velocity, rhs_old)),
        mesh=mesh,
        in_specs=(placed, placed),
        out_specs=(placed, placed),
        check_vma=False,
    )
```

```python
import functools
import math

import jax
import jax.numpy as jnp
import numpy as np
from jax import lax
from jax.experimental import pallas as pl
from jax.experimental.pallas import tpu as pltpu
from jax.sharding import PartitionSpec as P

TAPS = ((1, 45.0), (2, -9.0), (3, 1.0))
REACH = 3
TILE = 8
MIB = 1024 * 1024
F32 = jnp.float32


def decay_of(coupling):
    ratio = 0.5 / math.sqrt(coupling)
    theta = 2.0 * math.log(ratio + math.sqrt(ratio * ratio + 1.0))
    return theta, 1.0 / (coupling * (math.exp(theta) - math.exp(-theta)))


def round_table(count, blocks, theta, gain):
    rounds = blocks.bit_length() - 1
    wrap = gain / (1.0 - math.exp(-theta * count * blocks))
    factor = lambda steps: math.exp(-theta * count * (steps % blocks))
    table = np.zeros((blocks, 2 + 4 * (rounds - 1), 4))
    for block in range(blocks):
        takers = (block, block ^ 1)
        for i, taker in enumerate(takers):
            table[block, i, :2] = wrap * factor(taker - 1 - block)
            table[block, i, 2:] = wrap * factor(block - taker - 1)
        for k in range(1, rounds):
            size = 1 << (k - 1)
            start = ((block >> k) ^ 1) << (k - 1)
            lowest = 2 * start + (block & 1)
            highest = lowest + 2 * (size - 1)
            slot = 4 * k - 2
            shrink = math.exp(-theta * count * 2 * size)
            at_right = lowest > block
            table[block, slot] = (shrink, shrink, 1.0, 1.0) if at_right else (1.0, 1.0, shrink, shrink)
            table[block, slot + 1] = (1.0, 1.0, shrink, shrink) if at_right else (shrink, shrink, 1.0, 1.0)
            for i, taker in enumerate(takers):
                table[block, slot + 2 + i, :2] = wrap * factor(taker - 1 - highest)
                table[block, slot + 2 + i, 2:] = wrap * factor(lowest - taker - 1)
    return table


def scaled(table, slot, part, value):
    return value * table[slot, pl.ds(part, 1)]


def sums_kernel(theta, v_hbm, odd, fg, near_x, v, ends, sems, strip_sems):
    count, rows, lanes = v.shape[1:]
    chunk = TILE
    parts = count // chunk
    copies = {}
    for part in range(parts):
        for m in range(2):
            where = pl.ds(part * chunk, chunk)
            copies[part, m] = pltpu.make_async_copy(
                v_hbm.at[2 * m, where], v.at[m, where], sems.at[m, part]
            )
            copies[part, m].start()
    strips = []
    for i, start in enumerate((0, count - REACH)):
        strips.append(
            pltpu.make_async_copy(v_hbm.at[:, pl.ds(start, REACH)], ends.at[i], strip_sems.at[i])
        )
        strips[-1].start()
    for part in range(parts):
        for m in range(2):
            copies[part, m].wait()
            first = fg[m] if part else jnp.zeros((rows, lanes), F32)
            last = fg[2 + m] if part else jnp.zeros((rows, lanes), F32)
            for j in range(part * chunk, (part + 1) * chunk):
                cell = v[m, j]
                first = first * math.exp(-theta) + cell
                last = last + cell * math.exp(-theta * j)
            fg[m] = first
            fg[2 + m] = last
    for copy in strips:
        copy.wait()
    for c in range(3):
        for k in range(REACH):
            near_x[c, k] = jnp.where(odd[0:1] > 0.0, ends[0, c, k], ends[1, c, k])


def merge_kernel(k, table, held, got, *refs):
    out = refs[-1]
    for part in range(4):
        out[part] = scaled(table, 4 * k - 2, part, held[part]) + scaled(table, 4 * k - 1, part, got[part])


def flow(table, which, fg, received, part):
    total = scaled(table, which, part, fg[part])
    for k, got in enumerate(received, 1):
        total = total + scaled(table, 4 * k + which, part, got[part])
    return total


def outflow_kernel(rounds, table, fg, *refs):
    received, out = refs[: rounds - 1], refs[-1]
    for part in range(4):
        out[part] = flow(table, 1, fg, received, part)


def pack_kernel(v, odd, after, zhead, ztail, far_x):
    del after
    count, rows, lanes = v.shape[1:]
    for c in range(3):
        for k in range(REACH):
            far_x[c, k] = jnp.where(odd[0:1] > 0.0, v[c, count - REACH + k], v[c, k])
    flat = v.reshape(3 * count * rows, lanes)
    for target, base in ((zhead, 0), (ztail, rows - REACH)):
        for c in range(3):
            for k in range(REACH):
                target[k, c] = flat[pl.ds(c * count * rows + base + k, count, stride=rows), :]


def local_kernel(theta, gain, v, after, local):
    del after
    count, rows, lanes = v.shape[1:]
    ratio = math.exp(-theta)
    for m in range(2):

        def forward(x, run, m=m):
            run = run * ratio + v[2 * m, x]
            local[m, x] = run * gain
            return run

        lax.fori_loop(0, count, forward, jnp.zeros((rows, lanes), F32), unroll=4)

        def backward(i, run, m=m):
            x = count - 1 - i
            local[m, x] = local[m, x] + run * gain
            return (run + v[2 * m, x]) * ratio

        lax.fori_loop(0, count, backward, jnp.zeros((rows, lanes), F32), unroll=4)


def along_kernel(v, rhs, near_got, odd, inner, rim, base):
    count = v.shape[1]
    at_odd = odd[0:1]
    for c in range(3):

        def plane(x, carry, c=c):
            total = None
            for reach, tap in TAPS:
                term = (v[c, x + REACH + reach] - v[c, x + REACH - reach]) * (-tap / 60.0)
                total = term if total is None else total + term
            inner[c, x] = total
            return carry

        lax.fori_loop(0, count - 2 * REACH, plane, 0, unroll=2)
        for i, x in enumerate((*range(REACH), *range(count - REACH, count))):
            total = None
            share = at_odd if i < REACH else 1.0 - at_odd
            for reach, tap in TAPS:
                for side in (-1, 1):
                    at = x + side * reach
                    if 0 <= at < count:
                        term = v[c, at] * (-side * tap / 60.0)
                    else:
                        term = near_got[c, at % count % (count - REACH)] * (share * (-side * tap / 60.0))
                    total = term if total is None else total + term
            rim[c, i] = total

        def rest(x, carry, c=c):
            base[c, x] = v[c, x] - rhs[c, x] * (17.0 / 120.0)
            return carry

        lax.fori_loop(0, count, rest, 0, unroll=4)


def span_kernel(v, zleft, zright, span, low, high):
    count, rows, lanes = v.shape[1:]
    deep = 3 * TILE

    def differences(ref, lead, start, size):
        total = None
        for reach, tap in TAPS:
            up = ref[(*lead, pl.ds(start + reach, size))]
            down = ref[(*lead, pl.ds(start - reach, size))]
            term = (up - down) * (-tap / 60.0)
            total = term if total is None else total + term
        return total

    for c in range(3):
        for k in range(REACH):
            low.reshape(3 * count * deep, lanes)[
                pl.ds(c * count * deep + TILE - REACH + k, count, stride=deep), :
            ] = zleft[k, c]
            high.reshape(3 * count * deep, lanes)[
                pl.ds(c * count * deep + 2 * TILE + k, count, stride=deep), :
            ] = zright[k, c]

        def plane(x, carry, c=c):
            low[c, x, pl.ds(TILE, 2 * TILE)] = v[c, x, pl.ds(0, 2 * TILE)]
            high[c, x, pl.ds(0, 2 * TILE)] = v[c, x, pl.ds(rows - 2 * TILE, 2 * TILE)]
            span[c, x, pl.ds(TILE, rows - 2 * TILE)] = differences(v, (c, x), TILE, rows - 2 * TILE)
            span[c, x, pl.ds(0, TILE)] = differences(low, (c, x), TILE, TILE)
            span[c, x, pl.ds(rows - TILE, TILE)] = differences(high, (c, x), TILE, TILE)
            return carry

        lax.fori_loop(0, count, plane, 0, unroll=2)


def final_kernel(theta, rounds, table, odd, fg, *refs):
    received, mate = refs[: rounds - 1], refs[rounds - 1]
    far_got, inner, rim, span, local, base, new, conv, inflow, new_out, conv_out, sems = refs[rounds:]
    count = span.shape[1]
    chunk = 2
    ratio = math.exp(-theta)
    for part in range(4):
        inflow[part] = flow(table, 0, fg, received, part) + mate[part]

    def plane(x, rise, fall, gradients):
        smooth = [local[m, x] + inflow[m] * rise + inflow[2 + m] * fall for m in range(2)]
        for c in range(3):
            value = smooth[0] * gradients(c) + smooth[1] * span[c, x]
            conv_out[c, x] = value
            new_out[c, x] = base[c, x] + value * (5.0 / 24.0)

    def copies(x, size, sem):
        where = pl.ds(x, size)
        return [
            pltpu.make_async_copy(staged.at[:, where], out.at[:, where], sems.at[i, sem])
            for i, (staged, out) in enumerate(((new_out, new), (conv_out, conv)))
        ]

    chunks = (count - 2 * REACH) // chunk

    def body(i, carry):
        rise, fall = carry
        for at in range(chunk):
            x = REACH + i * chunk + at
            plane(x, rise * ratio**at, fall * ratio**-at, lambda c: inner[c, x - REACH])
        for copy in copies(REACH + i * chunk, chunk, i):
            copy.start()
        return rise * ratio**chunk, fall * ratio**-chunk

    lax.fori_loop(
        0,
        chunks,
        body,
        (jnp.float32(ratio ** (REACH + 1)), jnp.float32(ratio ** (count - REACH))),
    )
    for side, start in enumerate((0, count - REACH)):
        for at in range(REACH):
            x = start + at

            def gradients(c):
                total = rim[c, side * REACH + at]
                share = odd[0:1] if side else 1.0 - odd[0:1]
                for reach, tap in TAPS:
                    if x - reach < 0:
                        total = total + far_got[c, x - reach + REACH] * (share * (tap / 60.0))
                    if x + reach >= count:
                        total = total + far_got[c, x + reach - count] * (share * (-tap / 60.0))
                return total

            plane(x, ratio ** (x + 1), ratio ** (count - x), gradients)
        for copy in copies(start, REACH, chunks + side):
            copy.start()
    for i in range(chunks):
        for copy in copies(REACH + i * chunk, chunk, i):
            copy.wait()
    for side, start in enumerate((0, count - REACH)):
        for copy in copies(start, REACH, chunks + side):
            copy.wait()


def per_device(velocity, rhs_old):
    _, count, rows, lanes = velocity.shape
    blocks = lax.axis_size("gx")
    rounds = blocks.bit_length() - 1
    assert blocks == 1 << rounds
    filter_cells = count * blocks // 4
    theta, gain = decay_of(1.0 * filter_cells * filter_cells)
    kept = lambda *dims: pltpu.VMEM(dims, F32)
    near = lambda *arrays: [pltpu.with_memory_space_constraint(a, pltpu.VMEM) for a in arrays]
    far = lambda *arrays: [pltpu.with_memory_space_constraint(a, pltpu.HBM) for a in arrays]
    vmem = pl.BlockSpec(memory_space=pltpu.VMEM)
    hbm = pl.BlockSpec(memory_space=pltpu.HBM)
    dma = pltpu.SemaphoreType.DMA

    def call(kernel, name, inputs, in_specs, outputs, out_spec, scratch, mib, cost=0):
        return pl.pallas_call(
            kernel,
            cost_estimate=pl.CostEstimate(flops=int(cost*1e9), bytes_accessed=0, transcendentals=0) if cost else None,
            out_shape=outputs,
            in_specs=in_specs,
            out_specs=[out_spec] * len(outputs),
            scratch_shapes=scratch,
            compiler_params=pltpu.CompilerParams(vmem_limit_bytes=mib * MIB),
            name=name,
        )(*inputs)

    full = velocity.shape
    block = lax.axis_index("gx")
    odd = jnp.broadcast_to(1.0 - (block & 1).astype(F32), (TILE, lanes))
    entries = round_table(count, blocks, theta, gain)
    slots = entries.shape[1]
    table = lax.dynamic_index_in_dim(jnp.asarray(entries, F32), block, 0, keepdims=False)
    table = jnp.broadcast_to(table[:, :, None], (slots, 4, lanes))
    flip = lambda bit: [(i, i ^ bit) for i in range(blocks)]
    beyond = [(i, (i - 1 + 2 * (i % 2)) % blocks) for i in range(blocks)]
    ring = lambda axis, step: [(i, (i + step) % lax.axis_size(axis)) for i in range(lax.axis_size(axis))]

    fg, near_x = call(
        functools.partial(sums_kernel, theta),
        "sums",
        far(velocity) + near(odd),
        [hbm, vmem],
        [kept(4, rows, lanes), kept(3, REACH, rows, lanes)],
        vmem,
        [
            pltpu.VMEM((2, count, rows, lanes), F32),
            pltpu.VMEM((2, 3, REACH, rows, lanes), F32),
            dma((2, count // TILE)),
            dma((2,)),
        ],
        6,
    )
    (local,) = call(
        functools.partial(local_kernel, theta, gain),
        "local",
        near(velocity, fg),
        [vmem] * 2,
        [kept(2, *full[1:])],
        vmem,
        [],
        2,
        2,
    )
    received = [lax.ppermute(fg, "gx", flip(2))]
    near_got = lax.ppermute(near_x, "gx", beyond)
    held = fg
    for k in range(1, rounds - 1):
        (held,) = call(
            functools.partial(merge_kernel, k),
            "merge",
            near(table, held, received[-1]),
            [vmem] * 3,
            [kept(4, rows, lanes)],
            vmem,
            [],
            2,
        )
        received.append(lax.ppermute(held, "gx", flip(2 << k)))
        if k == 1:
            zhead, ztail, far_x = call(
                pack_kernel,
                "pack",
                near(velocity, odd, held),
                [vmem] * 3,
                [kept(REACH, 3, count, lanes)] * 2 + [kept(3, REACH, rows, lanes)],
                vmem,
                [],
                2,
            )
    zleft = lax.ppermute(ztail, "gz", ring("gz", 1))
    zright = lax.ppermute(zhead, "gz", ring("gz", -1))
    far_got = lax.ppermute(far_x, "gx", flip(1))
    (span,) = call(
        span_kernel,
        "span",
        near(velocity, zleft, zright),
        [vmem] * 3,
        [kept(*full)],
        vmem,
        [pltpu.VMEM((3, count, 3 * TILE, lanes), F32)] * 2,
        5,
        2,
    )
    inner, rim, base = call(
        along_kernel,
        "along",
        near(velocity, rhs_old, near_got, odd),
        [vmem] * 4,
        [kept(3, count - 2 * REACH, rows, lanes), kept(3, 2 * REACH, rows, lanes), kept(*full)],
        vmem,
        [],
        2,
        2,
    )
    (outflow,) = call(
        functools.partial(outflow_kernel, rounds),
        "outflow",
        near(table, fg, *received, rim),
        [vmem] * (rounds + 2),
        [kept(4, rows, lanes)],
        vmem,
        [],
        2,
    )
    mate = lax.ppermute(outflow, "gx", flip(1))
    inputs = near(table, odd, fg, *received, mate, far_got, inner, rim, span, local, base)
    return call(
        functools.partial(final_kernel, theta, rounds),
        "final",
        inputs,
        [vmem] * len(inputs),
        [jax.ShapeDtypeStruct(full, F32)] * 2,
        hbm,
        [pltpu.VMEM((4, rows, lanes), F32)]
        + [pltpu.VMEM(full, F32)] * 2
        + [dma((2, (count - 2 * REACH) // 2 + 2))],
        8,
    )


def solution(mesh):
    placed = P(None, "gx", "gz", None)
    return jax.shard_map(
        lambda velocity, rhs_old: tuple(per_device(velocity, rhs_old)),
        mesh=mesh,
        in_specs=(placed, placed),
        out_specs=(placed, placed),
        check_vma=False,
    )
```

```python
import functools
import math

import jax
import jax.numpy as jnp
import numpy as np
from jax import lax
from jax.experimental import pallas as pl
from jax.experimental.pallas import tpu as pltpu
from jax.sharding import PartitionSpec as P

TAPS = ((1, 45.0), (2, -9.0), (3, 1.0))
REACH = 3
TILE = 8
MIB = 1024 * 1024
F32 = jnp.float32


def decay_of(coupling):
    ratio = 0.5 / math.sqrt(coupling)
    theta = 2.0 * math.log(ratio + math.sqrt(ratio * ratio + 1.0))
    return theta, 1.0 / (coupling * (math.exp(theta) - math.exp(-theta)))


def round_table(count, blocks, theta, gain):
    rounds = blocks.bit_length() - 1
    wrap = gain / (1.0 - math.exp(-theta * count * blocks))
    factor = lambda steps: math.exp(-theta * count * (steps % blocks))
    table = np.zeros((blocks, 2 + 4 * (rounds - 1), 4))
    for block in range(blocks):
        takers = (block, block ^ 1)
        for i, taker in enumerate(takers):
            table[block, i, :2] = wrap * factor(taker - 1 - block)
            table[block, i, 2:] = wrap * factor(block - taker - 1)
        for k in range(1, rounds):
            size = 1 << (k - 1)
            start = ((block >> k) ^ 1) << (k - 1)
            lowest = 2 * start + (block & 1)
            highest = lowest + 2 * (size - 1)
            slot = 4 * k - 2
            shrink = math.exp(-theta * count * 2 * size)
            at_right = lowest > block
            table[block, slot] = (shrink, shrink, 1.0, 1.0) if at_right else (1.0, 1.0, shrink, shrink)
            table[block, slot + 1] = (1.0, 1.0, shrink, shrink) if at_right else (shrink, shrink, 1.0, 1.0)
            for i, taker in enumerate(takers):
                table[block, slot + 2 + i, :2] = wrap * factor(taker - 1 - highest)
                table[block, slot + 2 + i, 2:] = wrap * factor(lowest - taker - 1)
    return table


def scaled(table, slot, part, value):
    return value * table[slot, pl.ds(part, 1)]


def strips(v, lead, at_end, planes, out):
    for i, c in enumerate(lead):
        for k in range(REACH):
            out[i, k] = jnp.where(at_end, v[c, planes[1] + k], v[c, planes[0] + k])


def sums_kernel(theta, v_hbm, odd, fg, near_x, far_x, v, ends, sems, strip_sems):
    count, rows, lanes = v.shape[1:]
    chunk = TILE
    parts = count // chunk
    copies = {}
    for part in range(parts):
        for m in range(2):
            where = pl.ds(part * chunk, chunk)
            copies[part, m] = pltpu.make_async_copy(
                v_hbm.at[2 * m, where], v.at[m, where], sems.at[m, part]
            )
            copies[part, m].start()
    copies_ends = []
    for i, start in enumerate((0, count - REACH)):
        where = pl.ds(i * REACH, REACH)
        copies_ends.append(
            pltpu.make_async_copy(v_hbm.at[:, pl.ds(start, REACH)], ends.at[:, where], strip_sems.at[i])
        )
        copies_ends[-1].start()
    for part in range(parts):
        for m in range(2):
            copies[part, m].wait()
            first = fg[m] if part else jnp.zeros((rows, lanes), F32)
            last = fg[2 + m] if part else jnp.zeros((rows, lanes), F32)
            for j in range(part * chunk, (part + 1) * chunk):
                cell = v[m, j]
                first = first * math.exp(-theta) + cell
                last = last + cell * math.exp(-theta * j)
            fg[m] = first
            fg[2 + m] = last
    for copy in copies_ends:
        copy.wait()
    at_odd = odd[0:1] > 0.0
    strips(ends, range(3), ~at_odd, (0, REACH), near_x)
    strips(ends, range(far_x.shape[0]), at_odd, (0, REACH), far_x)


def merge_kernel(k, table, held, got, *refs):
    out = refs[-1]
    for part in range(4):
        out[part] = scaled(table, 4 * k - 2, part, held[part]) + scaled(table, 4 * k - 1, part, got[part])


def flow(table, which, fg, received, part):
    total = scaled(table, which, part, fg[part])
    for k, got in enumerate(received, 1):
        total = total + scaled(table, 4 * k + which, part, got[part])
    return total


def outflow_kernel(rounds, table, fg, *refs):
    received, out = refs[: rounds - 1], refs[-1]
    for part in range(4):
        out[part] = flow(table, 1, fg, received, part)


def pack_kernel(v, odd, after, zhead, ztail, *far_x):
    del after
    for out in far_x:
        strips(v, range(3 - out.shape[0], 3), odd[0:1] > 0.0, (0, v.shape[1] - REACH), out)
    count, rows, lanes = v.shape[1:]
    flat = v.reshape(3 * count * rows, lanes)
    for target, base in ((zhead, 0), (ztail, rows - REACH)):
        for c in range(3):
            for k in range(REACH):
                target[k, c] = flat[pl.ds(c * count * rows + base + k, count, stride=rows), :]


def local_kernel(theta, gain, v, after, local):
    del after
    count, rows, lanes = v.shape[1:]
    ratio = math.exp(-theta)
    for m in range(2):

        def forward(x, run, m=m):
            run = run * ratio + v[2 * m, x]
            local[m, x] = run * gain
            return run

        lax.fori_loop(0, count, forward, jnp.zeros((rows, lanes), F32), unroll=4)

        def backward(i, run, m=m):
            x = count - 1 - i
            local[m, x] = local[m, x] + run * gain
            return (run + v[2 * m, x]) * ratio

        lax.fori_loop(0, count, backward, jnp.zeros((rows, lanes), F32), unroll=4)


def along_kernel(v, rhs, after, inner, rim, base):
    del after
    count = v.shape[1]
    for c in range(3):

        def plane(x, carry, c=c):
            total = None
            for reach, tap in TAPS:
                term = (v[c, x + REACH + reach] - v[c, x + REACH - reach]) * (-tap / 60.0)
                total = term if total is None else total + term
            inner[c, x] = total
            return carry

        lax.fori_loop(0, count - 2 * REACH, plane, 0, unroll=2)
        for i, x in enumerate((*range(REACH), *range(count - REACH, count))):
            total = None
            for reach, tap in TAPS:
                for side in (-1, 1):
                    if 0 <= x + side * reach < count:
                        term = v[c, x + side * reach] * (-side * tap / 60.0)
                        total = term if total is None else total + term
            rim[c, i] = total

        def rest(x, carry, c=c):
            base[c, x] = v[c, x] - rhs[c, x] * (17.0 / 120.0)
            return carry

        lax.fori_loop(0, count, rest, 0, unroll=4)


def beyond_terms(cells, i, side):
    total = None
    for reach, tap in TAPS:
        at = i - reach + REACH if side == 0 else i + reach - REACH
        if 0 <= at < REACH:
            term = cells[at] * ((tap if side == 0 else -tap) / 60.0)
            total = term if total is None else total + term
    return total


def span_kernel(v, zleft, zright, span, low, high):
    count, rows, lanes = v.shape[1:]
    deep = 3 * TILE

    def differences(ref, lead, start, size):
        total = None
        for reach, tap in TAPS:
            up = ref[(*lead, pl.ds(start + reach, size))]
            down = ref[(*lead, pl.ds(start - reach, size))]
            term = (up - down) * (-tap / 60.0)
            total = term if total is None else total + term
        return total

    for c in range(3):
        for k in range(REACH):
            low.reshape(3 * count * deep, lanes)[
                pl.ds(c * count * deep + TILE - REACH + k, count, stride=deep), :
            ] = zleft[k, c]
            high.reshape(3 * count * deep, lanes)[
                pl.ds(c * count * deep + 2 * TILE + k, count, stride=deep), :
            ] = zright[k, c]

        def plane(x, carry, c=c):
            low[c, x, pl.ds(TILE, 2 * TILE)] = v[c, x, pl.ds(0, 2 * TILE)]
            high[c, x, pl.ds(0, 2 * TILE)] = v[c, x, pl.ds(rows - 2 * TILE, 2 * TILE)]
            span[c, x, pl.ds(TILE, rows - 2 * TILE)] = differences(v, (c, x), TILE, rows - 2 * TILE)
            span[c, x, pl.ds(0, TILE)] = differences(low, (c, x), TILE, TILE)
            span[c, x, pl.ds(rows - TILE, TILE)] = differences(high, (c, x), TILE, TILE)
            return carry

        lax.fori_loop(0, count, plane, 0, unroll=2)


def final_kernel(theta, rounds, table, odd, fg, *refs):
    received, mate = refs[: rounds - 1], refs[rounds - 1]
    inner, rim, span, local, base = refs[rounds : rounds + 5]
    near_hbm, *far_hbm = refs[rounds + 5 : -10]
    new, conv, inflow, whole, near_got, far_got, new_out, conv_out, sems, halo_sems = refs[-10:]
    count = span.shape[1]
    chunk = 2
    ratio = math.exp(-theta)
    halos = [pltpu.make_async_copy(near_hbm, near_got, halo_sems.at[0])]
    first = 0
    for i, source in enumerate(far_hbm, 1):
        size = source.shape[0]
        halos.append(pltpu.make_async_copy(source, far_got.at[pl.ds(first, size)], halo_sems.at[i]))
        first += size
    for copy in halos:
        copy.start()
    for part in range(4):
        inflow[part] = flow(table, 0, fg, received, part) + mate[part]

    def plane(x, rise, fall, gradient):
        smooth = [local[m, x] + inflow[m] * rise + inflow[2 + m] * fall for m in range(2)]
        for c in range(3):
            value = smooth[0] * gradient(c) + smooth[1] * span[c, x]
            conv_out[c, x] = value
            new_out[c, x] = base[c, x] + value * (5.0 / 24.0)

    def copies(x, planes, sem):
        where = pl.ds(x, planes)
        return [
            pltpu.make_async_copy(staged.at[:, where], out.at[:, where], sems.at[i, sem])
            for i, (staged, out) in enumerate(((new_out, new), (conv_out, conv)))
        ]

    chunks = (count - 2 * REACH) // chunk

    def body(i, carry):
        rise, fall = carry
        for step in range(chunk):
            at = i * chunk + step
            plane(at + REACH, rise * ratio**step, fall * ratio**-step, lambda c: inner[c, at])
        for copy in copies(REACH + i * chunk, chunk, i):
            copy.start()
        return rise * ratio**chunk, fall * ratio**-chunk

    start = (jnp.float32(ratio ** (REACH + 1)), jnp.float32(ratio ** (count - REACH)))
    lax.fori_loop(0, chunks, body, start)
    for copy in halos:
        copy.wait()
    at_odd = odd[0:1] > 0.0

    def ends_of(c, carry):
        near = [near_got[c, k] for k in range(REACH)]
        far = [far_got[c, k] for k in range(REACH)]
        left = [jnp.where(at_odd, near[k], far[k]) for k in range(REACH)]
        right = [jnp.where(at_odd, far[k], near[k]) for k in range(REACH)]
        for i in range(REACH):
            whole[c, i] = rim[c, i] + beyond_terms(left, i, 0)
            whole[c, REACH + i] = rim[c, REACH + i] + beyond_terms(right, i, 1)
        return carry

    lax.fori_loop(0, 3, ends_of, None)
    for side, begin in enumerate((0, count - REACH)):

        def edge(i, carry, side=side, begin=begin):
            rise, fall = carry
            plane(begin + i, rise, fall, lambda c: whole[c, side * REACH + i])
            return rise * ratio, fall / ratio

        start = (jnp.float32(ratio ** (begin + 1)), jnp.float32(ratio ** (count - begin)))
        lax.fori_loop(0, REACH, edge, start)
        for copy in copies(begin, REACH, chunks + side):
            copy.start()
    for i in range(chunks):
        for copy in copies(REACH + i * chunk, chunk, i):
            copy.wait()
    for side, begin in enumerate((0, count - REACH)):
        for copy in copies(begin, REACH, chunks + side):
            copy.wait()


def per_device(velocity, rhs_old):
    _, count, rows, lanes = velocity.shape
    blocks = lax.axis_size("gx")
    rounds = blocks.bit_length() - 1
    assert blocks == 1 << rounds
    filter_cells = count * blocks // 4
    theta, gain = decay_of(1.0 * filter_cells * filter_cells)
    kept = lambda *dims: pltpu.VMEM(dims, F32)
    near = lambda *arrays: [pltpu.with_memory_space_constraint(a, pltpu.VMEM) for a in arrays]
    far = lambda *arrays: [pltpu.with_memory_space_constraint(a, pltpu.HBM) for a in arrays]
    vmem = pl.BlockSpec(memory_space=pltpu.VMEM)
    hbm = pl.BlockSpec(memory_space=pltpu.HBM)
    anywhere = pl.BlockSpec(memory_space=pl.ANY)
    dma = pltpu.SemaphoreType.DMA

    def call(kernel, name, inputs, in_specs, outputs, out_spec, scratch, mib, cost=0, aliases={}):
        return pl.pallas_call(
            kernel,
            cost_estimate=pl.CostEstimate(flops=int(cost * 1e9), bytes_accessed=0, transcendentals=0) if cost else None,
            out_shape=outputs,
            input_output_aliases=aliases,
            in_specs=in_specs,
            out_specs=[out_spec] * len(outputs),
            scratch_shapes=scratch,
            compiler_params=pltpu.CompilerParams(vmem_limit_bytes=mib * MIB),
            name=name,
        )(*inputs)

    def plain(kernel, name, inputs, outputs, cost=0, scratch=(), mib=2):
        return call(kernel, name, near(*inputs), [vmem] * len(inputs), outputs, vmem, list(scratch), mib, cost)

    full = velocity.shape
    block = lax.axis_index("gx")
    odd = jnp.broadcast_to((block & 1).astype(F32), (TILE, lanes))
    entries = round_table(count, blocks, theta, gain)
    slots = entries.shape[1]
    table = lax.dynamic_index_in_dim(jnp.asarray(entries, F32), block, 0, keepdims=False)
    table = jnp.broadcast_to(table[:, :, None], (slots, 4, lanes))
    flip = lambda bit: [(i, i ^ bit) for i in range(blocks)]
    beyond = [(i, (i - 1 + 2 * (i % 2)) % blocks) for i in range(blocks)]
    ring = lambda axis, step: [(i, (i + step) % lax.axis_size(axis)) for i in range(lax.axis_size(axis))]
    sums = kept(4, rows, lanes)
    planes = lambda components: kept(components, REACH, rows, lanes)

    fg, near_x, far_x = call(
        functools.partial(sums_kernel, theta),
        "sums",
        far(velocity) + near(odd),
        [hbm, vmem],
        [sums, planes(3), planes(1)],
        vmem,
        [
            pltpu.VMEM((2, count, rows, lanes), F32),
            pltpu.VMEM((3, 2 * REACH, rows, lanes), F32),
            dma((2, count // TILE)),
            dma((2,)),
        ],
        6,
    )
    (local,) = plain(
        functools.partial(local_kernel, theta, gain), "local", [velocity, fg], [kept(2, *full[1:])], 2
    )
    received = [lax.ppermute(fg, "gx", flip(2))]
    far_got = lax.ppermute(far_x, "gx", beyond)
    near_got = lax.ppermute(near_x, "gx", flip(1))
    held = after = fg
    for k in range(1, rounds - 1):
        (held,) = plain(functools.partial(merge_kernel, k), "merge", [table, held, received[-1]], [sums])
        after = held if k == 1 else after
        received.append(lax.ppermute(held, "gx", flip(2 << k)))
    zhead, ztail, *far_x = plain(
        pack_kernel,
        "pack",
        [velocity, odd, after],
        [kept(REACH, 3, count, lanes)] * 2 + [planes(3 - 1)] * (1 < 3),
    )
    zleft = lax.ppermute(ztail, "gz", ring("gz", 1))
    zright = lax.ppermute(zhead, "gz", ring("gz", -1))
    far_parts = [far_got] + [lax.ppermute(x, "gx", beyond) for x in far_x]
    (outflow,) = plain(functools.partial(outflow_kernel, rounds), "outflow", [table, fg, *received, far_got], [sums])
    mate = lax.ppermute(outflow, "gx", flip(1))
    inner, rim, base = plain(
        along_kernel,
        "along",
        [velocity, rhs_old, after],
        [kept(3, count - 2 * REACH, rows, lanes), kept(3, 2 * REACH, rows, lanes), kept(*full)],
        2,
    )
    (span,) = plain(
        span_kernel,
        "span",
        [velocity, zleft, zright],
        [kept(*full)],
        0.5,
        [pltpu.VMEM((3, count, 3 * TILE, lanes), F32)] * 2,
        5,
    )
    sources = near(table, odd, fg, *received, mate, inner, rim, span, local, base)
    halos = [near_got, *far_parts]
    part = lambda *dims: pltpu.VMEM((*dims, rows, lanes), F32)
    return call(
        functools.partial(final_kernel, theta, rounds),
        "final",
        sources + halos,
        [vmem] * len(sources) + [anywhere] * len(halos),
        [jax.ShapeDtypeStruct(full, F32)] * 2,
        hbm,
        [part(4), part(3, 2 * REACH), part(3, REACH), part(3, REACH), part(3, count), part(3, count)]
        + [dma((2, (count - 2 * REACH) // 2 + 2)), dma((3,))],
        9,
    )


def solution(mesh):
    placed = P(None, "gx", "gz", None)
    return jax.shard_map(
        lambda velocity, rhs_old: tuple(per_device(velocity, rhs_old)),
        mesh=mesh,
        in_specs=(placed, placed),
        out_specs=(placed, placed),
        check_vma=False,
    )
```

```python
import functools
import math

import jax
import jax.numpy as jnp
import numpy as np
from jax import lax
from jax.experimental import pallas as pl
from jax.experimental.pallas import tpu as pltpu
from jax.sharding import PartitionSpec as P

TAPS = ((1, 45.0), (2, -9.0), (3, 1.0))
REACH = 3
TILE = 8
MIB = 1024 * 1024
F32 = jnp.float32


def decay_of(coupling):
    ratio = 0.5 / math.sqrt(coupling)
    theta = 2.0 * math.log(ratio + math.sqrt(ratio * ratio + 1.0))
    return theta, 1.0 / (coupling * (math.exp(theta) - math.exp(-theta)))


def round_table(count, blocks, theta, gain):
    rounds = blocks.bit_length() - 1
    wrap = gain / (1.0 - math.exp(-theta * count * blocks))
    factor = lambda steps: math.exp(-theta * count * (steps % blocks))
    table = np.zeros((blocks, 2 + 4 * (rounds - 1), 4))
    for block in range(blocks):
        takers = (block, block ^ 1)
        for i, taker in enumerate(takers):
            table[block, i, :2] = wrap * factor(taker - 1 - block)
            table[block, i, 2:] = wrap * factor(block - taker - 1)
        for k in range(1, rounds):
            size = 1 << (k - 1)
            start = ((block >> k) ^ 1) << (k - 1)
            lowest = 2 * start + (block & 1)
            highest = lowest + 2 * (size - 1)
            slot = 4 * k - 2
            shrink = math.exp(-theta * count * 2 * size)
            at_right = lowest > block
            table[block, slot] = (shrink, shrink, 1.0, 1.0) if at_right else (1.0, 1.0, shrink, shrink)
            table[block, slot + 1] = (1.0, 1.0, shrink, shrink) if at_right else (shrink, shrink, 1.0, 1.0)
            for i, taker in enumerate(takers):
                table[block, slot + 2 + i, :2] = wrap * factor(taker - 1 - highest)
                table[block, slot + 2 + i, 2:] = wrap * factor(lowest - taker - 1)
    return table


def scaled(table, slot, part, value):
    return value * table[slot, pl.ds(part, 1)]


def strips(v, lead, at_end, planes, out):
    for i, c in enumerate(lead):
        for k in range(REACH):
            out[i, k] = jnp.where(at_end, v[c, planes[1] + k], v[c, planes[0] + k])


def sums_kernel(theta, v_hbm, odd, fg, near_x, far_x, v, ends, sems, strip_sems):
    count, rows, lanes = v.shape[1:]
    chunk = TILE
    parts = count // chunk
    copies = {}
    for part in range(parts):
        for m in range(2):
            where = pl.ds(part * chunk, chunk)
            copies[part, m] = pltpu.make_async_copy(
                v_hbm.at[2 * m, where], v.at[m, where], sems.at[m, part]
            )
            copies[part, m].start()
    copies_ends = []
    for i, start in enumerate((0, count - REACH)):
        where = pl.ds(i * REACH, REACH)
        copies_ends.append(
            pltpu.make_async_copy(v_hbm.at[:, pl.ds(start, REACH)], ends.at[:, where], strip_sems.at[i])
        )
        copies_ends[-1].start()
    for part in range(parts):
        for m in range(2):
            copies[part, m].wait()
            first = fg[m] if part else jnp.zeros((rows, lanes), F32)
            last = fg[2 + m] if part else jnp.zeros((rows, lanes), F32)
            for j in range(part * chunk, (part + 1) * chunk):
                cell = v[m, j]
                first = first * math.exp(-theta) + cell
                last = last + cell * math.exp(-theta * j)
            fg[m] = first
            fg[2 + m] = last
    for copy in copies_ends:
        copy.wait()
    at_odd = odd[0:1] > 0.0
    strips(ends, range(3), ~at_odd, (0, REACH), near_x)
    strips(ends, range(far_x.shape[0]), at_odd, (0, REACH), far_x)


def merge_kernel(k, table, held, got, *refs):
    out = refs[-1]
    for part in range(4):
        out[part] = scaled(table, 4 * k - 2, part, held[part]) + scaled(table, 4 * k - 1, part, got[part])


def flow(table, which, fg, received, part):
    total = scaled(table, which, part, fg[part])
    for k, got in enumerate(received, 1):
        total = total + scaled(table, 4 * k + which, part, got[part])
    return total


def outflow_kernel(rounds, table, fg, *refs):
    received, out = refs[: rounds - 1], refs[-1]
    for part in range(4):
        out[part] = flow(table, 1, fg, received, part)


def pack_kernel(v, odd, after, zhead, ztail, *far_x):
    del after
    for out in far_x:
        strips(v, range(3 - out.shape[0], 3), odd[0:1] > 0.0, (0, v.shape[1] - REACH), out)
    count, rows, lanes = v.shape[1:]
    flat = v.reshape(3 * count * rows, lanes)
    for target, base in ((zhead, 0), (ztail, rows - REACH)):
        for c in range(3):
            for k in range(REACH):
                target[k, c] = flat[pl.ds(c * count * rows + base + k, count, stride=rows), :]


def local_kernel(theta, gain, v, after, local):
    del after
    count, rows, lanes = v.shape[1:]
    ratio = math.exp(-theta)
    for m in range(2):

        def forward(x, run, m=m):
            run = run * ratio + v[2 * m, x]
            local[m, x] = run * gain
            return run

        lax.fori_loop(0, count, forward, jnp.zeros((rows, lanes), F32), unroll=4)

        def backward(i, run, m=m):
            x = count - 1 - i
            local[m, x] = local[m, x] + run * gain
            return (run + v[2 * m, x]) * ratio

        lax.fori_loop(0, count, backward, jnp.zeros((rows, lanes), F32), unroll=4)


def along_kernel(v, rhs, after, inner, rim, base):
    del after
    count = v.shape[1]
    for c in range(3):

        def plane(x, carry, c=c):
            total = None
            for reach, tap in TAPS:
                term = (v[c, x + REACH + reach] - v[c, x + REACH - reach]) * (-tap / 60.0)
                total = term if total is None else total + term
            inner[c, x] = total
            return carry

        lax.fori_loop(0, count - 2 * REACH, plane, 0, unroll=2)
        for i, x in enumerate((*range(REACH), *range(count - REACH, count))):
            total = None
            for reach, tap in TAPS:
                for side in (-1, 1):
                    if 0 <= x + side * reach < count:
                        term = v[c, x + side * reach] * (-side * tap / 60.0)
                        total = term if total is None else total + term
            rim[c, i] = total

        def rest(x, carry, c=c):
            base[c, x] = v[c, x] - rhs[c, x] * (17.0 / 120.0)
            return carry

        lax.fori_loop(0, count, rest, 0, unroll=4)


def beyond_terms(cells, i, side):
    total = None
    for reach, tap in TAPS:
        at = i - reach + REACH if side == 0 else i + reach - REACH
        if 0 <= at < REACH:
            term = cells[at] * ((tap if side == 0 else -tap) / 60.0)
            total = term if total is None else total + term
    return total


def span_kernel(v, zleft, zright, span, low, high):
    count, rows, lanes = v.shape[1:]
    deep = 3 * TILE

    def differences(ref, lead, start, size):
        total = None
        for reach, tap in TAPS:
            up = ref[(*lead, pl.ds(start + reach, size))]
            down = ref[(*lead, pl.ds(start - reach, size))]
            term = (up - down) * (-tap / 60.0)
            total = term if total is None else total + term
        return total

    for c in range(3):
        for k in range(REACH):
            low.reshape(3 * count * deep, lanes)[
                pl.ds(c * count * deep + TILE - REACH + k, count, stride=deep), :
            ] = zleft[k, c]
            high.reshape(3 * count * deep, lanes)[
                pl.ds(c * count * deep + 2 * TILE + k, count, stride=deep), :
            ] = zright[k, c]

        def plane(x, carry, c=c):
            low[c, x, pl.ds(TILE, 2 * TILE)] = v[c, x, pl.ds(0, 2 * TILE)]
            high[c, x, pl.ds(0, 2 * TILE)] = v[c, x, pl.ds(rows - 2 * TILE, 2 * TILE)]
            span[c, x, pl.ds(TILE, rows - 2 * TILE)] = differences(v, (c, x), TILE, rows - 2 * TILE)
            span[c, x, pl.ds(0, TILE)] = differences(low, (c, x), TILE, TILE)
            span[c, x, pl.ds(rows - TILE, TILE)] = differences(high, (c, x), TILE, TILE)
            return carry

        lax.fori_loop(0, count, plane, 0, unroll=2)


def rim_kernel(rim, odd, near_hbm, *refs):
    *far_hbm, whole, near_got, far_got, sems = refs
    copies = [pltpu.make_async_copy(near_hbm, near_got, sems.at[0])]
    first = 0
    for i, source in enumerate(far_hbm, 1):
        size = source.shape[0]
        copies.append(pltpu.make_async_copy(source, far_got.at[pl.ds(first, size)], sems.at[i]))
        first += size
    for copy in copies:
        copy.start()
    for copy in copies:
        copy.wait()
    at_odd = odd[0:1] > 0.0

    def ends_of(c, carry):
        near = [near_got[c, k] for k in range(REACH)]
        far = [far_got[c, k] for k in range(REACH)]
        left = [jnp.where(at_odd, near[k], far[k]) for k in range(REACH)]
        right = [jnp.where(at_odd, far[k], near[k]) for k in range(REACH)]
        for i in range(REACH):
            whole[c, i] = rim[c, i] + beyond_terms(left, i, 0)
            whole[c, REACH + i] = rim[c, REACH + i] + beyond_terms(right, i, 1)
        return carry

    lax.fori_loop(0, 3, ends_of, None)


def final_kernel(theta, rounds, table, fg, *refs):
    received, mate = refs[: rounds - 1], refs[rounds - 1]
    inner, whole, span, local, base, new, conv, inflow, new_out, conv_out, sems = refs[rounds:]
    count = span.shape[1]
    chunk = 2
    ratio = math.exp(-theta)
    for part in range(4):
        inflow[part] = flow(table, 0, fg, received, part) + mate[part]

    def plane(x, rise, fall, gradient):
        smooth = [local[m, x] + inflow[m] * rise + inflow[2 + m] * fall for m in range(2)]
        for c in range(3):
            value = smooth[0] * gradient(c) + smooth[1] * span[c, x]
            conv_out[c, x] = value
            new_out[c, x] = base[c, x] + value * (5.0 / 24.0)

    def copies(x, planes, sem):
        where = pl.ds(x, planes)
        return [
            pltpu.make_async_copy(staged.at[:, where], out.at[:, where], sems.at[i, sem])
            for i, (staged, out) in enumerate(((new_out, new), (conv_out, conv)))
        ]

    chunks = (count - 2 * REACH) // chunk

    def body(i, carry):
        rise, fall = carry
        for step in range(chunk):
            at = i * chunk + step
            plane(at + REACH, rise * ratio**step, fall * ratio**-step, lambda c: inner[c, at])
        for copy in copies(REACH + i * chunk, chunk, i):
            copy.start()
        return rise * ratio**chunk, fall * ratio**-chunk

    start = (jnp.float32(ratio ** (REACH + 1)), jnp.float32(ratio ** (count - REACH)))
    lax.fori_loop(0, chunks, body, start)
    for side, begin in enumerate((0, count - REACH)):

        def edge(i, carry, side=side, begin=begin):
            rise, fall = carry
            plane(begin + i, rise, fall, lambda c: whole[c, side * REACH + i])
            return rise * ratio, fall / ratio

        start = (jnp.float32(ratio ** (begin + 1)), jnp.float32(ratio ** (count - begin)))
        lax.fori_loop(0, REACH, edge, start)
        for copy in copies(begin, REACH, chunks + side):
            copy.start()
    for i in range(chunks):
        for copy in copies(REACH + i * chunk, chunk, i):
            copy.wait()
    for side, begin in enumerate((0, count - REACH)):
        for copy in copies(begin, REACH, chunks + side):
            copy.wait()


def per_device(velocity, rhs_old):
    _, count, rows, lanes = velocity.shape
    blocks = lax.axis_size("gx")
    rounds = blocks.bit_length() - 1
    assert blocks == 1 << rounds
    filter_cells = count * blocks // 4
    theta, gain = decay_of(1.0 * filter_cells * filter_cells)
    kept = lambda *dims: pltpu.VMEM(dims, F32)
    near = lambda *arrays: [pltpu.with_memory_space_constraint(a, pltpu.VMEM) for a in arrays]
    far = lambda *arrays: [pltpu.with_memory_space_constraint(a, pltpu.HBM) for a in arrays]
    vmem = pl.BlockSpec(memory_space=pltpu.VMEM)
    hbm = pl.BlockSpec(memory_space=pltpu.HBM)
    anywhere = pl.BlockSpec(memory_space=pl.ANY)
    dma = pltpu.SemaphoreType.DMA

    def call(kernel, name, inputs, in_specs, outputs, out_spec, scratch, mib, cost=0, aliases={}):
        return pl.pallas_call(
            kernel,
            cost_estimate=pl.CostEstimate(flops=int(cost * 1e9), bytes_accessed=0, transcendentals=0) if cost else None,
            out_shape=outputs,
            input_output_aliases=aliases,
            in_specs=in_specs,
            out_specs=[out_spec] * len(outputs),
            scratch_shapes=scratch,
            compiler_params=pltpu.CompilerParams(vmem_limit_bytes=mib * MIB),
            name=name,
        )(*inputs)

    def plain(kernel, name, inputs, outputs, cost=0, scratch=(), mib=2):
        return call(kernel, name, near(*inputs), [vmem] * len(inputs), outputs, vmem, list(scratch), mib, cost)

    full = velocity.shape
    block = lax.axis_index("gx")
    odd = jnp.broadcast_to((block & 1).astype(F32), (TILE, lanes))
    entries = round_table(count, blocks, theta, gain)
    slots = entries.shape[1]
    table = lax.dynamic_index_in_dim(jnp.asarray(entries, F32), block, 0, keepdims=False)
    table = jnp.broadcast_to(table[:, :, None], (slots, 4, lanes))
    flip = lambda bit: [(i, i ^ bit) for i in range(blocks)]
    beyond = [(i, (i - 1 + 2 * (i % 2)) % blocks) for i in range(blocks)]
    ring = lambda axis, step: [(i, (i + step) % lax.axis_size(axis)) for i in range(lax.axis_size(axis))]
    sums = kept(4, rows, lanes)
    planes = lambda components: kept(components, REACH, rows, lanes)

    fg, near_x, far_x = call(
        functools.partial(sums_kernel, theta),
        "sums",
        far(velocity) + near(odd),
        [hbm, vmem],
        [sums, planes(3), planes(1)],
        vmem,
        [
            pltpu.VMEM((2, count, rows, lanes), F32),
            pltpu.VMEM((3, 2 * REACH, rows, lanes), F32),
            dma((2, count // TILE)),
            dma((2,)),
        ],
        6,
    )
    (local,) = plain(
        functools.partial(local_kernel, theta, gain), "local", [velocity, fg], [kept(2, *full[1:])], 2
    )
    received = [lax.ppermute(fg, "gx", flip(2))]
    far_got = lax.ppermute(far_x, "gx", beyond)
    near_got = lax.ppermute(near_x, "gx", flip(1))
    held = after = fg
    for k in range(1, rounds - 1):
        (held,) = plain(functools.partial(merge_kernel, k), "merge", [table, held, received[-1]], [sums])
        after = held if k == 1 else after
        received.append(lax.ppermute(held, "gx", flip((4 << k) - 2)))
    zhead, ztail, *far_x = plain(
        pack_kernel,
        "pack",
        [velocity, odd, after],
        [kept(REACH, 3, count, lanes)] * 2 + [planes(3 - 1)] * (1 < 3),
    )
    zleft = lax.ppermute(ztail, "gz", ring("gz", 1))
    zright = lax.ppermute(zhead, "gz", ring("gz", -1))
    far_parts = [far_got] + [lax.ppermute(x, "gx", beyond) for x in far_x]
    (outflow,) = plain(functools.partial(outflow_kernel, rounds), "outflow", [table, fg, *received, far_got], [sums])
    mate = lax.ppermute(outflow, "gx", flip(1))
    inner, rim, base = plain(
        along_kernel,
        "along",
        [velocity, rhs_old, after],
        [kept(3, count - 2 * REACH, rows, lanes), kept(3, 2 * REACH, rows, lanes), kept(*full)],
        2,
    )
    (span,) = plain(
        span_kernel,
        "span",
        [velocity, zleft, zright],
        [kept(*full)],
        0.5,
        [pltpu.VMEM((3, count, 3 * TILE, lanes), F32)] * 2,
        5,
    )
    part = lambda *dims: pltpu.VMEM((*dims, rows, lanes), F32)
    halos = [near_got, *far_parts]
    (rim,) = call(
        rim_kernel,
        "rim",
        near(rim, odd) + halos,
        [vmem] * 2 + [anywhere] * len(halos),
        [kept(3, 2 * REACH, rows, lanes)],
        vmem,
        [part(3, REACH)] * 2 + [dma((3,))],
        3,
        0.1,
    )
    sources = near(table, fg, *received, mate, inner, rim, span, local, base)
    return call(
        functools.partial(final_kernel, theta, rounds),
        "final",
        sources,
        [vmem] * len(sources),
        [jax.ShapeDtypeStruct(full, F32)] * 2,
        hbm,
        [part(4), part(3, count), part(3, count)] + [dma((2, (count - 2 * REACH) // 2 + 2))],
        8,
    )


def solution(mesh):
    placed = P(None, "gx", "gz", None)
    return jax.shard_map(
        lambda velocity, rhs_old: tuple(per_device(velocity, rhs_old)),
        mesh=mesh,
        in_specs=(placed, placed),
        out_specs=(placed, placed),
        check_vma=False,
    )
```

```python
import functools
import math

import jax
import jax.numpy as jnp
import numpy as np
from jax import lax
from jax.experimental import pallas as pl
from jax.experimental.pallas import tpu as pltpu
from jax.sharding import PartitionSpec as P

TAPS = ((1, 45.0), (2, -9.0), (3, 1.0))
REACH = 3
TILE = 8
MIB = 1024 * 1024
F32 = jnp.float32


def decay_of(coupling):
    ratio = 0.5 / math.sqrt(coupling)
    theta = 2.0 * math.log(ratio + math.sqrt(ratio * ratio + 1.0))
    return theta, 1.0 / (coupling * (math.exp(theta) - math.exp(-theta)))


def round_table(count, blocks, theta, gain):
    rounds = blocks.bit_length() - 1
    wrap = gain / (1.0 - math.exp(-theta * count * blocks))
    factor = lambda steps: math.exp(-theta * count * (steps % blocks))
    table = np.zeros((blocks, 2 + 4 * (rounds - 1), 4))
    for block in range(blocks):
        takers = (block, block ^ 1)
        for i, taker in enumerate(takers):
            table[block, i, :2] = wrap * factor(taker - 1 - block)
            table[block, i, 2:] = wrap * factor(block - taker - 1)
        for k in range(1, rounds):
            size = 1 << (k - 1)
            start = ((block >> k) ^ 1) << (k - 1)
            lowest = 2 * start + (block & 1)
            highest = lowest + 2 * (size - 1)
            slot = 4 * k - 2
            shrink = math.exp(-theta * count * 2 * size)
            at_right = lowest > block
            table[block, slot] = (shrink, shrink, 1.0, 1.0) if at_right else (1.0, 1.0, shrink, shrink)
            table[block, slot + 1] = (1.0, 1.0, shrink, shrink) if at_right else (shrink, shrink, 1.0, 1.0)
            for i, taker in enumerate(takers):
                table[block, slot + 2 + i, :2] = wrap * factor(taker - 1 - highest)
                table[block, slot + 2 + i, 2:] = wrap * factor(lowest - taker - 1)
    return table


def scaled(table, slot, part, value):
    return value * table[slot, pl.ds(part, 1)]


def strips(v, lead, at_end, planes, out):
    for i, c in enumerate(lead):
        for k in range(REACH):
            out[i, k] = jnp.where(at_end, v[c, planes[1] + k], v[c, planes[0] + k])


def sums_kernel(theta, v_hbm, odd, fg, near_x, far_x, v, ends, sems, strip_sems):
    count, rows, lanes = v.shape[1:]
    chunk = TILE
    parts = count // chunk
    copies = {}
    for part in range(parts):
        for m in range(2):
            where = pl.ds(part * chunk, chunk)
            copies[part, m] = pltpu.make_async_copy(
                v_hbm.at[2 * m, where], v.at[m, where], sems.at[m, part]
            )
            copies[part, m].start()
    copies_ends = []
    for i, start in enumerate((0, count - REACH)):
        where = pl.ds(i * REACH, REACH)
        copies_ends.append(
            pltpu.make_async_copy(v_hbm.at[:, pl.ds(start, REACH)], ends.at[:, where], strip_sems.at[i])
        )
        copies_ends[-1].start()
    for part in range(parts):
        for m in range(2):
            copies[part, m].wait()
            first = fg[m] if part else jnp.zeros((rows, lanes), F32)
            last = fg[2 + m] if part else jnp.zeros((rows, lanes), F32)
            for j in range(part * chunk, (part + 1) * chunk):
                cell = v[m, j]
                first = first * math.exp(-theta) + cell
                last = last + cell * math.exp(-theta * j)
            fg[m] = first
            fg[2 + m] = last
    for copy in copies_ends:
        copy.wait()
    at_odd = odd[0:1] > 0.0
    strips(ends, range(3), ~at_odd, (0, REACH), near_x)
    strips(ends, range(far_x.shape[0]), at_odd, (0, REACH), far_x)


def merge_kernel(k, table, held, got, *refs):
    out = refs[-1]
    for part in range(4):
        out[part] = scaled(table, 4 * k - 2, part, held[part]) + scaled(table, 4 * k - 1, part, got[part])


def flow(table, which, fg, received, part):
    total = scaled(table, which, part, fg[part])
    for k, got in enumerate(received, 1):
        total = total + scaled(table, 4 * k + which, part, got[part])
    return total


def outflow_kernel(rounds, table, fg, *refs):
    received, out = refs[: rounds - 1], refs[-1]
    for part in range(4):
        out[part] = flow(table, 1, fg, received, part)


def pack_kernel(v, after, zhead, ztail):
    del after
    count, rows, lanes = v.shape[1:]
    flat = v.reshape(3 * count * rows, lanes)
    for target, base in ((zhead, 0), (ztail, rows - REACH)):
        for c in range(3):
            for k in range(REACH):
                target[k, c] = flat[pl.ds(c * count * rows + base + k, count, stride=rows), :]


def local_kernel(theta, gain, v, after, local):
    del after
    count, rows, lanes = v.shape[1:]
    ratio = math.exp(-theta)
    for m in range(2):

        def forward(x, run, m=m):
            run = run * ratio + v[2 * m, x]
            local[m, x] = run * gain
            return run

        lax.fori_loop(0, count, forward, jnp.zeros((rows, lanes), F32), unroll=4)

        def backward(i, run, m=m):
            x = count - 1 - i
            local[m, x] = local[m, x] + run * gain
            return (run + v[2 * m, x]) * ratio

        lax.fori_loop(0, count, backward, jnp.zeros((rows, lanes), F32), unroll=4)


def along_kernel(v, rhs, odd, after, *refs):
    count = v.shape[1]
    inner, rim, base, *far_x = refs if len(refs) == 3 else refs[1:]
    for out in far_x:
        strips(v, range(3 - out.shape[0], 3), odd[0:1] > 0.0, (0, count - REACH), out)
    for c in range(3):

        def plane(x, carry, c=c):
            total = None
            for reach, tap in TAPS:
                term = (v[c, x + REACH + reach] - v[c, x + REACH - reach]) * (-tap / 60.0)
                total = term if total is None else total + term
            inner[c, x] = total
            return carry

        lax.fori_loop(0, count - 2 * REACH, plane, 0, unroll=2)
        for i, x in enumerate((*range(REACH), *range(count - REACH, count))):
            total = None
            for reach, tap in TAPS:
                for side in (-1, 1):
                    if 0 <= x + side * reach < count:
                        term = v[c, x + side * reach] * (-side * tap / 60.0)
                        total = term if total is None else total + term
            rim[c, i] = total

        def rest(x, carry, c=c):
            base[c, x] = v[c, x] - rhs[c, x] * (17.0 / 120.0)
            return carry

        lax.fori_loop(0, count, rest, 0, unroll=4)


def beyond_terms(cells, i, side):
    total = None
    for reach, tap in TAPS:
        at = i - reach + REACH if side == 0 else i + reach - REACH
        if 0 <= at < REACH:
            term = cells[at] * ((tap if side == 0 else -tap) / 60.0)
            total = term if total is None else total + term
    return total


def span_kernel(v, zleft, zright, span, low, high):
    count, rows, lanes = v.shape[1:]
    deep = 3 * TILE

    def differences(ref, lead, start, size):
        total = None
        for reach, tap in TAPS:
            up = ref[(*lead, pl.ds(start + reach, size))]
            down = ref[(*lead, pl.ds(start - reach, size))]
            term = (up - down) * (-tap / 60.0)
            total = term if total is None else total + term
        return total

    for c in range(3):
        for k in range(REACH):
            low.reshape(3 * count * deep, lanes)[
                pl.ds(c * count * deep + TILE - REACH + k, count, stride=deep), :
            ] = zleft[k, c]
            high.reshape(3 * count * deep, lanes)[
                pl.ds(c * count * deep + 2 * TILE + k, count, stride=deep), :
            ] = zright[k, c]

        def plane(x, carry, c=c):
            low[c, x, pl.ds(TILE, 2 * TILE)] = v[c, x, pl.ds(0, 2 * TILE)]
            high[c, x, pl.ds(0, 2 * TILE)] = v[c, x, pl.ds(rows - 2 * TILE, 2 * TILE)]
            span[c, x, pl.ds(TILE, rows - 2 * TILE)] = differences(v, (c, x), TILE, rows - 2 * TILE)
            span[c, x, pl.ds(0, TILE)] = differences(low, (c, x), TILE, TILE)
            span[c, x, pl.ds(rows - TILE, TILE)] = differences(high, (c, x), TILE, TILE)
            return carry

        lax.fori_loop(0, count, plane, 0, unroll=2)


def final_kernel(theta, rounds, table, odd, fg, *refs):
    received, mate = refs[: rounds - 1], refs[rounds - 1]
    inner, rim, span, local, base = refs[rounds : rounds + 5]
    near_hbm, *far_hbm = refs[rounds + 5 : -10]
    new, conv, inflow, whole, near_got, far_got, new_out, conv_out, sems, halo_sems = refs[-10:]
    count = span.shape[1]
    chunk = 2
    ratio = math.exp(-theta)
    halos = [pltpu.make_async_copy(near_hbm, near_got, halo_sems.at[0])]
    first = 0
    for i, source in enumerate(far_hbm, 1):
        size = source.shape[0]
        halos.append(pltpu.make_async_copy(source, far_got.at[pl.ds(first, size)], halo_sems.at[i]))
        first += size
    for copy in halos:
        copy.start()
    for part in range(4):
        inflow[part] = flow(table, 0, fg, received, part) + mate[part]

    def plane(x, rise, fall, gradient):
        smooth = [local[m, x] + inflow[m] * rise + inflow[2 + m] * fall for m in range(2)]
        for c in range(3):
            value = smooth[0] * gradient(c) + smooth[1] * span[c, x]
            conv_out[c, x] = value
            new_out[c, x] = base[c, x] + value * (5.0 / 24.0)

    def copies(x, planes, sem):
        where = pl.ds(x, planes)
        return [
            pltpu.make_async_copy(staged.at[:, where], out.at[:, where], sems.at[i, sem])
            for i, (staged, out) in enumerate(((new_out, new), (conv_out, conv)))
        ]

    chunks = (count - 2 * REACH) // chunk

    def body(i, carry):
        rise, fall = carry
        for step in range(chunk):
            at = i * chunk + step
            plane(at + REACH, rise * ratio**step, fall * ratio**-step, lambda c: inner[c, at])
        for copy in copies(REACH + i * chunk, chunk, i):
            copy.start()
        return rise * ratio**chunk, fall * ratio**-chunk

    start = (jnp.float32(ratio ** (REACH + 1)), jnp.float32(ratio ** (count - REACH)))
    lax.fori_loop(0, chunks, body, start)
    for copy in halos:
        copy.wait()
    at_odd = odd[0:1] > 0.0

    def ends_of(c, carry):
        near = [near_got[c, k] for k in range(REACH)]
        far = [far_got[c, k] for k in range(REACH)]
        left = [jnp.where(at_odd, near[k], far[k]) for k in range(REACH)]
        right = [jnp.where(at_odd, far[k], near[k]) for k in range(REACH)]
        for i in range(REACH):
            whole[c, i] = rim[c, i] + beyond_terms(left, i, 0)
            whole[c, REACH + i] = rim[c, REACH + i] + beyond_terms(right, i, 1)
        return carry

    lax.fori_loop(0, 3, ends_of, None)
    for side, begin in enumerate((0, count - REACH)):

        def edge(i, carry, side=side, begin=begin):
            rise, fall = carry
            plane(begin + i, rise, fall, lambda c: whole[c, side * REACH + i])
            return rise * ratio, fall / ratio

        start = (jnp.float32(ratio ** (begin + 1)), jnp.float32(ratio ** (count - begin)))
        lax.fori_loop(0, REACH, edge, start)
        for copy in copies(begin, REACH, chunks + side):
            copy.start()
    for i in range(chunks):
        for copy in copies(REACH + i * chunk, chunk, i):
            copy.wait()
    for side, begin in enumerate((0, count - REACH)):
        for copy in copies(begin, REACH, chunks + side):
            copy.wait()


def per_device(velocity, rhs_old):
    _, count, rows, lanes = velocity.shape
    blocks = lax.axis_size("gx")
    rounds = blocks.bit_length() - 1
    assert blocks == 1 << rounds
    filter_cells = count * blocks // 4
    theta, gain = decay_of(1.0 * filter_cells * filter_cells)
    kept = lambda *dims: pltpu.VMEM(dims, F32)
    near = lambda *arrays: [pltpu.with_memory_space_constraint(a, pltpu.VMEM) for a in arrays]
    far = lambda *arrays: [pltpu.with_memory_space_constraint(a, pltpu.HBM) for a in arrays]
    vmem = pl.BlockSpec(memory_space=pltpu.VMEM)
    hbm = pl.BlockSpec(memory_space=pltpu.HBM)
    anywhere = pl.BlockSpec(memory_space=pl.ANY)
    dma = pltpu.SemaphoreType.DMA

    def call(kernel, name, inputs, in_specs, outputs, out_spec, scratch, mib, cost=0, aliases={}):
        return pl.pallas_call(
            kernel,
            cost_estimate=pl.CostEstimate(flops=int(cost * 1e9), bytes_accessed=0, transcendentals=0) if cost else None,
            out_shape=outputs,
            input_output_aliases=aliases,
            in_specs=in_specs,
            out_specs=[out_spec] * len(outputs),
            scratch_shapes=scratch,
            compiler_params=pltpu.CompilerParams(vmem_limit_bytes=mib * MIB),
            name=name,
        )(*inputs)

    def plain(kernel, name, inputs, outputs, cost=0, scratch=(), mib=2):
        return call(kernel, name, near(*inputs), [vmem] * len(inputs), outputs, vmem, list(scratch), mib, cost)

    full = velocity.shape
    block = lax.axis_index("gx")
    odd = jnp.broadcast_to((block & 1).astype(F32), (TILE, lanes))
    entries = round_table(count, blocks, theta, gain)
    slots = entries.shape[1]
    table = lax.dynamic_index_in_dim(jnp.asarray(entries, F32), block, 0, keepdims=False)
    table = jnp.broadcast_to(table[:, :, None], (slots, 4, lanes))
    flip = lambda bit: [(i, i ^ bit) for i in range(blocks)]
    beyond = [(i, (i - 1 + 2 * (i % 2)) % blocks) for i in range(blocks)]
    ring = lambda axis, step: [(i, (i + step) % lax.axis_size(axis)) for i in range(lax.axis_size(axis))]
    sums = kept(4, rows, lanes)
    planes = lambda components: kept(components, REACH, rows, lanes)

    fg, near_x, far_x = call(
        functools.partial(sums_kernel, theta),
        "sums",
        far(velocity) + near(odd),
        [hbm, vmem],
        [sums, planes(3), planes(3)],
        vmem,
        [
            pltpu.VMEM((2, count, rows, lanes), F32),
            pltpu.VMEM((3, 2 * REACH, rows, lanes), F32),
            dma((2, count // TILE)),
            dma((2,)),
        ],
        6,
    )
    (local,) = plain(
        functools.partial(local_kernel, theta, gain), "local", [velocity, fg], [kept(2, *full[1:])], 0.5
    )
    received = [lax.ppermute(fg, "gx", flip(2))]
    far_got = lax.ppermute(far_x, "gx", beyond)
    near_got = lax.ppermute(near_x, "gx", flip(1))
    held = after = fg
    for k in range(1, rounds - 1):
        (held,) = plain(functools.partial(merge_kernel, k), "merge", [table, held, received[-1]], [sums])
        after = held if k == 1 else after
        received.append(lax.ppermute(held, "gx", flip((4 << k) - 2)))
    zhead, ztail = plain(pack_kernel, "pack", [velocity, after], [kept(REACH, 3, count, lanes)] * 2)
    zleft = lax.ppermute(ztail, "gz", ring("gz", 1))
    zright = lax.ppermute(zhead, "gz", ring("gz", -1))
    inner, rim, base, *far_x = plain(
        along_kernel,
        "along",
        [velocity, rhs_old, odd, after],
        [kept(3, count - 2 * REACH, rows, lanes), kept(3, 2 * REACH, rows, lanes), kept(*full)],
        1,
    )
    far_parts = [far_got] + [lax.ppermute(x, "gx", beyond) for x in far_x]
    (outflow,) = plain(functools.partial(outflow_kernel, rounds), "outflow", [table, fg, *received, rim], [sums])
    mate = lax.ppermute(outflow, "gx", flip(1))
    (span,) = plain(
        span_kernel,
        "span",
        [velocity, zleft, zright],
        [kept(*full)],
        1,
        [pltpu.VMEM((3, count, 3 * TILE, lanes), F32)] * 2,
        5,
    )
    sources = near(table, odd, fg, *received, mate, inner, rim, span, local, base)
    halos = [near_got, *far_parts]
    part = lambda *dims: pltpu.VMEM((*dims, rows, lanes), F32)
    return call(
        functools.partial(final_kernel, theta, rounds),
        "final",
        sources + halos,
        [vmem] * len(sources) + [anywhere] * len(halos),
        [jax.ShapeDtypeStruct(full, F32)] * 2,
        hbm,
        [part(4), part(3, 2 * REACH), part(3, REACH), part(3, REACH), part(3, count), part(3, count)]
        + [dma((2, (count - 2 * REACH) // 2 + 2)), dma((3,))],
        9,
    )


def solution(mesh):
    placed = P(None, "gx", "gz", None)
    return jax.shard_map(
        lambda velocity, rhs_old: tuple(per_device(velocity, rhs_old)),
        mesh=mesh,
        in_specs=(placed, placed),
        out_specs=(placed, placed),
        check_vma=False,
    )
```

```python
import functools
import math

import jax
import jax.numpy as jnp
import numpy as np
from jax import lax
from jax.experimental import pallas as pl
from jax.experimental.pallas import tpu as pltpu
from jax.sharding import PartitionSpec as P

TAPS = ((1, 45.0), (2, -9.0), (3, 1.0))
REACH = 3
TILE = 8
MIB = 1024 * 1024
F32 = jnp.float32


def decay_of(coupling):
    ratio = 0.5 / math.sqrt(coupling)
    theta = 2.0 * math.log(ratio + math.sqrt(ratio * ratio + 1.0))
    return theta, 1.0 / (coupling * (math.exp(theta) - math.exp(-theta)))


def round_table(count, blocks, theta, gain):
    rounds = blocks.bit_length() - 1
    wrap = gain / (1.0 - math.exp(-theta * count * blocks))
    factor = lambda steps: math.exp(-theta * count * (steps % blocks))
    table = np.zeros((blocks, 2 + 4 * (rounds - 1), 4))
    for block in range(blocks):
        takers = (block, block ^ 1)
        for i, taker in enumerate(takers):
            table[block, i, :2] = wrap * factor(taker - 1 - block)
            table[block, i, 2:] = wrap * factor(block - taker - 1)
        for k in range(1, rounds):
            size = 1 << (k - 1)
            start = ((block >> k) ^ 1) << (k - 1)
            lowest = 2 * start + (block & 1)
            highest = lowest + 2 * (size - 1)
            slot = 4 * k - 2
            shrink = math.exp(-theta * count * 2 * size)
            at_right = lowest > block
            table[block, slot] = (shrink, shrink, 1.0, 1.0) if at_right else (1.0, 1.0, shrink, shrink)
            table[block, slot + 1] = (1.0, 1.0, shrink, shrink) if at_right else (shrink, shrink, 1.0, 1.0)
            for i, taker in enumerate(takers):
                table[block, slot + 2 + i, :2] = wrap * factor(taker - 1 - highest)
                table[block, slot + 2 + i, 2:] = wrap * factor(lowest - taker - 1)
    return table


def scaled(table, slot, part, value):
    return value * table[slot, pl.ds(part, 1)]


def strips(v, lead, at_end, planes, out):
    for i, c in enumerate(lead):
        for k in range(REACH):
            out[i, k] = jnp.where(at_end, v[c, planes[1] + k], v[c, planes[0] + k])


def sums_kernel(theta, v_hbm, odd, fg, near_x, far_x, v, ends, sems, strip_sems):
    count, rows, lanes = v.shape[1:]
    chunk = TILE
    parts = count // chunk
    copies = {}
    for part in range(parts):
        for m in range(2):
            where = pl.ds(part * chunk, chunk)
            copies[part, m] = pltpu.make_async_copy(
                v_hbm.at[2 * m, where], v.at[m, where], sems.at[m, part]
            )
            copies[part, m].start()
    copies_ends = []
    for i, start in enumerate((0, count - REACH)):
        where = pl.ds(i * REACH, REACH)
        copies_ends.append(
            pltpu.make_async_copy(v_hbm.at[:, pl.ds(start, REACH)], ends.at[:, where], strip_sems.at[i])
        )
        copies_ends[-1].start()
    for part in range(parts):
        for m in range(2):
            copies[part, m].wait()
            first = fg[m] if part else jnp.zeros((rows, lanes), F32)
            last = fg[2 + m] if part else jnp.zeros((rows, lanes), F32)
            for j in range(part * chunk, (part + 1) * chunk):
                cell = v[m, j]
                first = first * math.exp(-theta) + cell
                last = last + cell * math.exp(-theta * j)
            fg[m] = first
            fg[2 + m] = last
    for copy in copies_ends:
        copy.wait()
    at_odd = odd[0:1] > 0.0
    strips(ends, range(3), ~at_odd, (0, REACH), near_x)
    strips(ends, range(far_x.shape[0]), at_odd, (0, REACH), far_x)


def merge_kernel(k, table, held, got, *refs):
    out = refs[-1]
    for part in range(4):
        out[part] = scaled(table, 4 * k - 2, part, held[part]) + scaled(table, 4 * k - 1, part, got[part])


def flow(table, which, fg, received, part):
    total = scaled(table, which, part, fg[part])
    for k, got in enumerate(received, 1):
        total = total + scaled(table, 4 * k + which, part, got[part])
    return total


def outflow_kernel(rounds, table, fg, *refs):
    received, out = refs[: rounds - 1], refs[-1]
    for part in range(4):
        out[part] = flow(table, 1, fg, received, part)


def pack_kernel(v, after, zhead, ztail):
    del after
    count, rows, lanes = v.shape[1:]
    flat = v.reshape(3 * count * rows, lanes)
    for target, base in ((zhead, 0), (ztail, rows - REACH)):
        for c in range(3):
            for k in range(REACH):
                target[k, c] = flat[pl.ds(c * count * rows + base + k, count, stride=rows), :]


def local_kernel(theta, gain, v, after, local):
    del after
    count, rows, lanes = v.shape[1:]
    ratio = math.exp(-theta)
    for m in range(2):

        def forward(x, run, m=m):
            run = run * ratio + v[2 * m, x]
            local[m, x] = run * gain
            return run

        lax.fori_loop(0, count, forward, jnp.zeros((rows, lanes), F32), unroll=4)

        def backward(i, run, m=m):
            x = count - 1 - i
            local[m, x] = local[m, x] + run * gain
            return (run + v[2 * m, x]) * ratio

        lax.fori_loop(0, count, backward, jnp.zeros((rows, lanes), F32), unroll=4)


def along_kernel(v, rhs, odd, after, *refs):
    count = v.shape[1]
    inner, rim, base, *far_x = refs if len(refs) == 3 else refs[1:]
    for out in far_x:
        strips(v, range(3 - out.shape[0], 3), odd[0:1] > 0.0, (0, count - REACH), out)
    for c in range(3):

        def plane(x, carry, c=c):
            total = None
            for reach, tap in TAPS:
                term = (v[c, x + REACH + reach] - v[c, x + REACH - reach]) * (-tap / 60.0)
                total = term if total is None else total + term
            inner[c, x] = total
            return carry

        lax.fori_loop(0, count - 2 * REACH, plane, 0, unroll=2)
        for i, x in enumerate((*range(REACH), *range(count - REACH, count))):
            total = None
            for reach, tap in TAPS:
                for side in (-1, 1):
                    if 0 <= x + side * reach < count:
                        term = v[c, x + side * reach] * (-side * tap / 60.0)
                        total = term if total is None else total + term
            rim[c, i] = total

        def rest(x, carry, c=c):
            base[c, x] = v[c, x] - rhs[c, x] * (17.0 / 120.0)
            return carry

        lax.fori_loop(0, count, rest, 0, unroll=4)


def beyond_terms(cells, i, side):
    total = None
    for reach, tap in TAPS:
        at = i - reach + REACH if side == 0 else i + reach - REACH
        if 0 <= at < REACH:
            term = cells[at] * ((tap if side == 0 else -tap) / 60.0)
            total = term if total is None else total + term
    return total


def span_kernel(v, zleft, zright, span, low, high):
    count, rows, lanes = v.shape[1:]
    deep = 3 * TILE

    def differences(ref, lead, start, size):
        total = None
        for reach, tap in TAPS:
            up = ref[(*lead, pl.ds(start + reach, size))]
            down = ref[(*lead, pl.ds(start - reach, size))]
            term = (up - down) * (-tap / 60.0)
            total = term if total is None else total + term
        return total

    for c in range(3):
        for k in range(REACH):
            low.reshape(3 * count * deep, lanes)[
                pl.ds(c * count * deep + TILE - REACH + k, count, stride=deep), :
            ] = zleft[k, c]
            high.reshape(3 * count * deep, lanes)[
                pl.ds(c * count * deep + 2 * TILE + k, count, stride=deep), :
            ] = zright[k, c]

        def plane(x, carry, c=c):
            low[c, x, pl.ds(TILE, 2 * TILE)] = v[c, x, pl.ds(0, 2 * TILE)]
            high[c, x, pl.ds(0, 2 * TILE)] = v[c, x, pl.ds(rows - 2 * TILE, 2 * TILE)]
            span[c, x, pl.ds(TILE, rows - 2 * TILE)] = differences(v, (c, x), TILE, rows - 2 * TILE)
            span[c, x, pl.ds(0, TILE)] = differences(low, (c, x), TILE, TILE)
            span[c, x, pl.ds(rows - TILE, TILE)] = differences(high, (c, x), TILE, TILE)
            return carry

        lax.fori_loop(0, count, plane, 0, unroll=2)


def rim_kernel(rim, odd, near_hbm, *refs):
    *far_hbm, whole, near_got, far_got, sems = refs
    copies = [pltpu.make_async_copy(near_hbm, near_got, sems.at[0])]
    first = 0
    for i, source in enumerate(far_hbm, 1):
        size = source.shape[0]
        copies.append(pltpu.make_async_copy(source, far_got.at[pl.ds(first, size)], sems.at[i]))
        first += size
    for copy in copies:
        copy.start()
    for copy in copies:
        copy.wait()
    at_odd = odd[0:1] > 0.0

    def ends_of(c, carry):
        near = [near_got[c, k] for k in range(REACH)]
        far = [far_got[c, k] for k in range(REACH)]
        left = [jnp.where(at_odd, near[k], far[k]) for k in range(REACH)]
        right = [jnp.where(at_odd, far[k], near[k]) for k in range(REACH)]
        for i in range(REACH):
            whole[c, i] = rim[c, i] + beyond_terms(left, i, 0)
            whole[c, REACH + i] = rim[c, REACH + i] + beyond_terms(right, i, 1)
        return carry

    lax.fori_loop(0, 3, ends_of, None)


def final_kernel(theta, rounds, table, fg, *refs):
    received, mate = refs[: rounds - 1], refs[rounds - 1]
    inner, whole, span, local, base, new, conv, inflow, new_out, conv_out, sems = refs[rounds:]
    count = span.shape[1]
    chunk = 2
    ratio = math.exp(-theta)
    for part in range(4):
        inflow[part] = flow(table, 0, fg, received, part) + mate[part]

    def plane(x, rise, fall, gradient):
        smooth = [local[m, x] + inflow[m] * rise + inflow[2 + m] * fall for m in range(2)]
        for c in range(3):
            value = smooth[0] * gradient(c) + smooth[1] * span[c, x]
            conv_out[c, x] = value
            new_out[c, x] = base[c, x] + value * (5.0 / 24.0)

    def copies(x, planes, sem):
        where = pl.ds(x, planes)
        return [
            pltpu.make_async_copy(staged.at[:, where], out.at[:, where], sems.at[i, sem])
            for i, (staged, out) in enumerate(((new_out, new), (conv_out, conv)))
        ]

    chunks = (count - 2 * REACH) // chunk

    def body(i, carry):
        rise, fall = carry
        for step in range(chunk):
            at = i * chunk + step
            plane(at + REACH, rise * ratio**step, fall * ratio**-step, lambda c: inner[c, at])
        for copy in copies(REACH + i * chunk, chunk, i):
            copy.start()
        return rise * ratio**chunk, fall * ratio**-chunk

    start = (jnp.float32(ratio ** (REACH + 1)), jnp.float32(ratio ** (count - REACH)))
    lax.fori_loop(0, chunks, body, start)
    for side, begin in enumerate((0, count - REACH)):

        def edge(i, carry, side=side, begin=begin):
            rise, fall = carry
            plane(begin + i, rise, fall, lambda c: whole[c, side * REACH + i])
            return rise * ratio, fall / ratio

        start = (jnp.float32(ratio ** (begin + 1)), jnp.float32(ratio ** (count - begin)))
        lax.fori_loop(0, REACH, edge, start)
        for copy in copies(begin, REACH, chunks + side):
            copy.start()
    for i in range(chunks):
        for copy in copies(REACH + i * chunk, chunk, i):
            copy.wait()
    for side, begin in enumerate((0, count - REACH)):
        for copy in copies(begin, REACH, chunks + side):
            copy.wait()


def per_device(velocity, rhs_old):
    _, count, rows, lanes = velocity.shape
    blocks = lax.axis_size("gx")
    rounds = blocks.bit_length() - 1
    assert blocks == 1 << rounds
    filter_cells = count * blocks // 4
    theta, gain = decay_of(1.0 * filter_cells * filter_cells)
    kept = lambda *dims: pltpu.VMEM(dims, F32)
    near = lambda *arrays: [pltpu.with_memory_space_constraint(a, pltpu.VMEM) for a in arrays]
    far = lambda *arrays: [pltpu.with_memory_space_constraint(a, pltpu.HBM) for a in arrays]
    vmem = pl.BlockSpec(memory_space=pltpu.VMEM)
    hbm = pl.BlockSpec(memory_space=pltpu.HBM)
    anywhere = pl.BlockSpec(memory_space=pl.ANY)
    dma = pltpu.SemaphoreType.DMA

    def call(kernel, name, inputs, in_specs, outputs, out_spec, scratch, mib, cost=0, aliases={}):
        return pl.pallas_call(
            kernel,
            cost_estimate=pl.CostEstimate(flops=int(cost * 1e9), bytes_accessed=0, transcendentals=0) if cost else None,
            out_shape=outputs,
            input_output_aliases=aliases,
            in_specs=in_specs,
            out_specs=[out_spec] * len(outputs),
            scratch_shapes=scratch,
            compiler_params=pltpu.CompilerParams(vmem_limit_bytes=mib * MIB),
            name=name,
        )(*inputs)

    def plain(kernel, name, inputs, outputs, cost=0, scratch=(), mib=2):
        return call(kernel, name, near(*inputs), [vmem] * len(inputs), outputs, vmem, list(scratch), mib, cost)

    full = velocity.shape
    block = lax.axis_index("gx")
    odd = jnp.broadcast_to((block & 1).astype(F32), (TILE, lanes))
    entries = round_table(count, blocks, theta, gain)
    slots = entries.shape[1]
    table = lax.dynamic_index_in_dim(jnp.asarray(entries, F32), block, 0, keepdims=False)
    table = jnp.broadcast_to(table[:, :, None], (slots, 4, lanes))
    flip = lambda bit: [(i, i ^ bit) for i in range(blocks)]
    beyond = [(i, (i - 1 + 2 * (i % 2)) % blocks) for i in range(blocks)]
    ring = lambda axis, step: [(i, (i + step) % lax.axis_size(axis)) for i in range(lax.axis_size(axis))]
    sums = kept(4, rows, lanes)
    planes = lambda components: kept(components, REACH, rows, lanes)

    fg, near_x, far_x = call(
        functools.partial(sums_kernel, theta),
        "sums",
        far(velocity) + near(odd),
        [hbm, vmem],
        [sums, planes(3), planes(3)],
        vmem,
        [
            pltpu.VMEM((2, count, rows, lanes), F32),
            pltpu.VMEM((3, 2 * REACH, rows, lanes), F32),
            dma((2, count // TILE)),
            dma((2,)),
        ],
        6,
    )
    (local,) = plain(
        functools.partial(local_kernel, theta, gain), "local", [velocity, fg], [kept(2, *full[1:])], 0.5
    )
    received = [lax.ppermute(fg, "gx", flip(2))]
    far_got = lax.ppermute(far_x, "gx", beyond)
    near_got = lax.ppermute(near_x, "gx", flip(1))
    held = after = fg
    for k in range(1, rounds - 1):
        (held,) = plain(functools.partial(merge_kernel, k), "merge", [table, held, received[-1]], [sums])
        after = held if k == 1 else after
        received.append(lax.ppermute(held, "gx", flip((4 << k) - 2)))
    zhead, ztail = plain(pack_kernel, "pack", [velocity, after], [kept(REACH, 3, count, lanes)] * 2)
    zleft = lax.ppermute(ztail, "gz", ring("gz", 1))
    zright = lax.ppermute(zhead, "gz", ring("gz", -1))
    inner, rim, base, *far_x = plain(
        along_kernel,
        "along",
        [velocity, rhs_old, odd, after],
        [kept(3, count - 2 * REACH, rows, lanes), kept(3, 2 * REACH, rows, lanes), kept(*full)],
        1,
    )
    far_parts = [far_got] + [lax.ppermute(x, "gx", beyond) for x in far_x]
    (outflow,) = plain(functools.partial(outflow_kernel, rounds), "outflow", [table, fg, *received, rim], [sums])
    mate = lax.ppermute(outflow, "gx", flip(1))
    (span,) = plain(
        span_kernel,
        "span",
        [velocity, zleft, zright],
        [kept(*full)],
        1,
        [pltpu.VMEM((3, count, 3 * TILE, lanes), F32)] * 2,
        5,
    )
    part = lambda *dims: pltpu.VMEM((*dims, rows, lanes), F32)
    halos = [near_got, *far_parts]
    (rim,) = call(
        rim_kernel,
        "rim",
        near(rim, odd) + halos,
        [vmem] * 2 + [anywhere] * len(halos),
        [kept(3, 2 * REACH, rows, lanes)],
        vmem,
        [part(3, REACH)] * 2 + [dma((3,))],
        3,
        0.1,
    )
    sources = near(table, fg, *received, mate, inner, rim, span, local, base)
    return call(
        functools.partial(final_kernel, theta, rounds),
        "final",
        sources,
        [vmem] * len(sources),
        [jax.ShapeDtypeStruct(full, F32)] * 2,
        hbm,
        [part(4), part(3, count), part(3, count)] + [dma((2, (count - 2 * REACH) // 2 + 2))],
        8,
    )


def solution(mesh):
    placed = P(None, "gx", "gz", None)
    return jax.shard_map(
        lambda velocity, rhs_old: tuple(per_device(velocity, rhs_old)),
        mesh=mesh,
        in_specs=(placed, placed),
        out_specs=(placed, placed),
        check_vma=False,
    )
```
